256 devices in a mesh: dp: 8 (over z_hi, x), seq: 32 (over y, z_lo, core).
Axes of the slice: x: 4, y: 4, z: 8 (z_hi: 2, z_lo: 4; z = z_hi * 4 + z_lo), core: 2. Of those that a mesh axis runs over, the one named last changes fastest.
Arguments:
- tokens: bfloat16 [8, 96, 96, 1152], P('dp', 'seq'), may hold values from -36 to 36
- timestep: int32 [8], P('dp'), may hold values from 0 to 15, as said below
- time_table: float32 [16, 3, 1152], replicated, may hold values from -3 to 3
- block_tables: float32 [2, 3, 1152], replicated, may hold values from -3 to 3
- qk_gains: float32 [2, 2, 72], replicated, may hold values from 0.1 to 1.9
- qkv_weight: bfloat16 [2, 1152, 1728], replicated, may hold values from -0.1875 to 0.1875
- proj_weight: bfloat16 [2, 1152, 576], replicated, may hold values from -0.25 to 0.25
- cotangent: bfloat16 [8, 96, 96, 1152], P('dp', 'seq'), may hold values from -6 to 6
Outputs:
- block_out: bfloat16 [8, 96, 96, 1152], P('dp', 'seq')
- token_grad: bfloat16 [8, 96, 96, 1152], P('dp', 'seq')
- qkv_grad: float32 [2, 1152, 1728], P(None, 'seq', 'dp')
- proj_grad: float32 [2, 1152, 576], P(None, 'seq', 'dp')
- table_grad: float32 [2, 3, 1152], replicated
- gain_grad: float32 [2, 2, 72], replicated
The draws below stay inside these ranges and needn't reach their ends.
Inputs may be any that keep to these rules, and one draw needn't show every extreme that they name: The clips' timesteps are distinct, and one clip has timestep 16 - 1.
All inputs are finite; a program needn't handle non-finite values.
Results may differ from the reference program's by a relative error of at most 0.034.
Values may be sent and summed in bfloat16 or wider, within the bound.
A program may use at most 128 MiB of HBM per device.

```python
import math
import jax
import jax.numpy as jnp
from jax import lax

D = 1152
HD = 72
HW = 576
STEPS = 16
CLIPS = 8
FRAMES = 96
SPATIAL = 96
N_SEQ = 32


def draw_tokens(key, part):
    key = jax.random.fold_in(key, 11)
    subkeys = jax.random.split(key, 3)
    extent = (CLIPS, FRAMES, SPATIAL, D)
    row_scale = jnp.exp(jax.random.uniform(subkeys[1], (CLIPS, FRAMES, SPATIAL, 1), jnp.float32, -1.2, 1.1))
    col_scale = jnp.exp(jax.random.uniform(subkeys[2], (1, 1, 1, D), jnp.float32, -1.2, 1.1))
    baseline = jnp.clip(jax.random.normal(subkeys[0], extent, jnp.float32), -4.0, 4.0)
    return jnp.clip(baseline * row_scale * col_scale, -36.0, 36.0).astype(jnp.bfloat16)


def draw_timestep(key, part):
    key = jax.random.fold_in(key, 23)
    subkeys = jax.random.split(key, 2)
    others = jax.random.permutation(subkeys[0], jnp.arange(STEPS - 1, dtype=jnp.int32))[:CLIPS - 1]
    chosen = jnp.concatenate([jnp.full((1,), STEPS - 1, jnp.int32), others.astype(jnp.int32)])
    order = jax.random.permutation(subkeys[1], jnp.arange(CLIPS, dtype=jnp.int32))
    return chosen[order].astype(jnp.int32)


def strengthened(result, rng, source, target, shards_of, factor):
    owner, partner = [(jnp.arange(result.shape[axis_at]) // (result.shape[axis_at] // shards_of)).reshape([-1 if axis == axis_at else 1 for axis in range(result.ndim)]) for axis_at in (source, target)]
    chosen = jax.random.permutation(rng, shards_of)[partner]
    strong = (owner == chosen) | (owner == (partner + shards_of // 2) % shards_of)
    return jnp.where(strong, factor * result, result)


def block_levels(rng, shape, cuts, low, top_value):
    loudness, own = 1.0, jax.random.fold_in(rng, 6)
    for axis_at, shards_of in cuts:
        draws = jnp.exp(jax.random.uniform(jax.random.fold_in(own, axis_at), (shards_of,), jnp.float32, low / len(cuts), top_value / len(cuts)))
        loudness = loudness * jnp.repeat(draws, shape[axis_at] // shards_of).reshape([-1 if axis == axis_at else 1 for axis in range(len(shape))])
    return loudness


def bell_draw(stream_key, shape, width, reach, cuts=(), kind=jnp.bfloat16):
    result = jax.random.normal(stream_key, shape, jnp.float32) * width
    if len(cuts) > 0:
        result = block_levels(stream_key, shape, cuts, -0.22, 0.18) * result
    return jnp.clip(result, min=-reach, max=reach).astype(kind)


def heavy_noise(own_key, dims, deviation, reach, cuts, heavy, kind=jnp.bfloat16):
    result = deviation * jax.random.normal(own_key, dims, jnp.float32)
    if cuts:
        result = result * block_levels(own_key, dims, cuts, -0.22, 0.18)
    return jnp.clip(strengthened(result, jax.random.fold_in(own_key, 3), *heavy), -reach, reach).astype(kind)


def setup_inputs(seed: int = 0) -> dict:
    arg_keys = jax.random.split(jax.random.key(seed), 9)
    return {
        "tokens": draw_tokens(jax.random.fold_in(arg_keys[8], 71), 0),
        "timestep": draw_timestep(jax.random.fold_in(arg_keys[8], 71), 0),
        "time_table": bell_draw(arg_keys[2], (STEPS, 3, D), 0.5, 3.0, (), jnp.float32),
        "block_tables": bell_draw(arg_keys[3], (2, 3, D), 0.5, 3.0, (), jnp.float32),
        "qk_gains": jnp.clip(1.0 + 0.18 * jax.random.normal(arg_keys[4], (2, 2, HD), jnp.float32), 0.1, 1.9),
        "qkv_weight": bell_draw(arg_keys[5], (2, D, 3 * HW), D ** -0.5, 0.1875),
        "proj_weight": bell_draw(arg_keys[6], (2, D, HW), HW ** -0.5, 0.25),
        "cotangent": heavy_noise(arg_keys[7], (CLIPS, SPATIAL, FRAMES, D), 1.0, 6.0, ((0, 8), (1, 32)), (1, 3, 32, 2.75)),
    }


EPSILON = 1e-06

def round_half(values):
    return lax.optimization_barrier(values.astype(jnp.bfloat16))

def product(form, former, latter):
    return jnp.einsum(form, former.astype(jnp.float32), latter.astype(jnp.float32))

def rope_tables(length, depth):
    halfway = depth // 2
    counter = jnp.arange(halfway, dtype=jnp.float32)
    frequency = jnp.power(jnp.float32(10000.0), -2.0 * counter / depth)
    angles = jnp.arange(length, dtype=jnp.float32)[:, None] * frequency[None, :]
    return (jnp.cos(angles), jnp.sin(angles))

def rotate(vectors, rope_pair, orient):
    cosine = rope_pair[0][None, :, None, :]
    sine = orient * rope_pair[1][None, :, None, :]
    halfway = vectors.shape[-1] // 2
    leading = vectors[..., :halfway]
    trailing = vectors[..., halfway:]
    return jnp.concatenate([leading * cosine - trailing * sine, trailing * cosine + leading * sine], -1)

def head_norm(raw_heads, gain_vec):
    widened = raw_heads.astype(jnp.float32)
    factor = lax.rsqrt(lax.optimization_barrier(jnp.mean(widened * widened, -1, keepdims=True)) + EPSILON)
    unit_vec = widened * factor
    return (unit_vec, factor, unit_vec * gain_vec)

def unit_back(unit_grad, unit_vec, factor):
    return factor * (unit_grad - unit_vec * lax.optimization_barrier(jnp.mean(unit_grad * unit_vec, -1, keepdims=True)))

def layer_forward(tokens_in, modulation, gain_pair, qkv_matrix, proj_matrix, rope_pair):
    groups, length, features = tokens_in.shape
    head_width = proj_matrix.shape[1]
    head_count = head_width // HD
    widened = tokens_in.astype(jnp.float32)
    center = widened - lax.optimization_barrier(jnp.mean(widened, -1, keepdims=True))
    inverse = lax.rsqrt(lax.optimization_barrier(jnp.mean(center * center, -1, keepdims=True)) + EPSILON)
    normed = center * inverse
    hidden = round_half(normed * (1.0 + modulation[1]) + modulation[0])
    qkv_half = round_half(jnp.dot(hidden, qkv_matrix, preferred_element_type=jnp.float32))
    parted = qkv_half.reshape(groups, length, 3, head_count, HD)
    query_unit, query_factor, query_rot = head_norm(parted[:, :, 0], gain_pair[0])
    key_unit, key_factor, key_rot = head_norm(parted[:, :, 1], gain_pair[1])
    if rope_pair is not None:
        query_rot = rotate(query_rot, rope_pair, 1.0)
        key_rot = rotate(key_rot, rope_pair, 1.0)
    query_half = round_half(query_rot)
    key_half = round_half(key_rot)
    scores = product('glhd,gmhd->ghlm', query_half, key_half) * (1.0 / math.sqrt(HD))
    exponent = jnp.exp(scores)
    attention = exponent / lax.optimization_barrier(jnp.sum(exponent, -1, keepdims=True))
    attention_half = round_half(attention)
    attended = round_half(product('ghlm,gmhd->glhd', attention_half, parted[:, :, 2]))
    attended = attended.reshape(groups, length, head_width)
    projected = lax.dot_general(attended, proj_matrix, (((2,), (1,)), ((), ())), preferred_element_type=jnp.float32)
    output = (widened + modulation[2] * projected).astype(jnp.bfloat16)
    stored = (normed, inverse, hidden, qkv_half, query_unit, query_factor, key_unit, key_factor, query_half, key_half, attention, attended, projected)
    return (output, stored)

def layer_backward(grad_out, stored, modulation, gain_pair, qkv_matrix, proj_matrix, rope_pair):
    normed, inverse, hidden, qkv_half, query_unit, query_factor, key_unit, key_factor, query_half, key_half, attention, attended, projected = stored
    groups, length, features = grad_out.shape
    head_width = proj_matrix.shape[1]
    head_count = head_width // HD
    upstream = grad_out.astype(jnp.float32)
    gate_grad = lax.optimization_barrier(jnp.sum(upstream * projected, (0, 1)))
    proj_in = round_half(upstream * modulation[2])
    attended_grad = round_half(jnp.dot(proj_in, proj_matrix, preferred_element_type=jnp.float32))
    attended_grad = attended_grad.reshape(groups, length, head_count, HD)
    values = qkv_half.reshape(groups, length, 3, head_count, HD)[:, :, 2]
    attention_half = round_half(attention)
    softmax_grad = product('glhd,gmhd->ghlm', attended_grad, values)
    value_grad = product('ghlm,glhd->gmhd', attention_half, attended_grad)
    score_grad = round_half(attention * (softmax_grad - lax.optimization_barrier(jnp.sum(softmax_grad * attention, -1, keepdims=True))))
    query_grad = product('ghlm,gmhd->glhd', score_grad, key_half) * (1.0 / math.sqrt(HD))
    key_grad = product('ghlm,glhd->gmhd', score_grad, query_half) * (1.0 / math.sqrt(HD))
    if rope_pair is not None:
        query_grad = rotate(query_grad, rope_pair, -1.0)
        key_grad = rotate(key_grad, rope_pair, -1.0)
    query_gain = lax.optimization_barrier(jnp.sum(query_grad * query_unit, (0, 1, 2)))
    key_gain = lax.optimization_barrier(jnp.sum(key_grad * key_unit, (0, 1, 2)))
    query_back = unit_back(query_grad * gain_pair[0], query_unit, query_factor)
    key_back = unit_back(key_grad * gain_pair[1], key_unit, key_factor)
    qkv_back = round_half(jnp.stack([query_back, key_back, value_grad], 2).reshape(groups, length, 3 * head_width))
    hidden_grad = lax.dot_general(qkv_back, qkv_matrix, (((2,), (1,)), ((), ())), preferred_element_type=jnp.float32)
    shift_grad = lax.optimization_barrier(jnp.sum(hidden_grad, (0, 1)))
    scale_grad = lax.optimization_barrier(jnp.sum(hidden_grad * normed, (0, 1)))
    normed_grad = hidden_grad * (1.0 + modulation[1])
    input_grad = upstream + inverse * (normed_grad - lax.optimization_barrier(jnp.mean(normed_grad, -1, keepdims=True)) - normed * lax.optimization_barrier(jnp.mean(normed_grad * normed, -1, keepdims=True)))
    table_terms = jnp.stack([shift_grad, scale_grad, gate_grad])
    gain_terms = jnp.stack([query_gain, key_gain])
    return (input_grad.astype(jnp.bfloat16), table_terms, gain_terms, (hidden, qkv_back, proj_in, attended))

def shard_sums(former, latter):
    left_rows = former.reshape(N_SEQ, -1, former.shape[-1])
    right_rows = latter.reshape(N_SEQ, -1, latter.shape[-1])

    def accumulate(running, pieces):
        term = jnp.einsum('ra,rb->ab', pieces[0].astype(jnp.float32), pieces[1].astype(jnp.float32))
        return (running + round_half(term).astype(jnp.float32), None)
    initial = jnp.zeros((former.shape[-1], latter.shape[-1]), jnp.float32)
    return lax.scan(accumulate, initial, (left_rows, right_rows))[0]

def reference(tokens, timestep, time_table, block_tables, qk_gains, qkv_weight, proj_weight, cotangent):
    rope_pair = rope_tables(FRAMES, HD)

    def clip_step(running, inputs):
        clip_tokens, clip_index, clip_cotangent = inputs
        modulation = block_tables + time_table[clip_index]
        middle, spatial_stored = layer_forward(clip_tokens, modulation[0], qk_gains[0], qkv_weight[0], proj_weight[0], None)
        block_out, temporal_stored = layer_forward(jnp.transpose(middle, (1, 0, 2)), modulation[1], qk_gains[1], qkv_weight[1], proj_weight[1], rope_pair)
        middle_grad, table_late, gain_late, parts_late = layer_backward(clip_cotangent, temporal_stored, modulation[1], qk_gains[1], qkv_weight[1], proj_weight[1], rope_pair)
        token_grad, table_early, gain_early, parts_early = layer_backward(jnp.transpose(middle_grad, (1, 0, 2)), spatial_stored, modulation[0], qk_gains[0], qkv_weight[0], proj_weight[0], None)
        qkv_sum, proj_sum, table_sum, gain_sum = running
        qkv_sum = qkv_sum + jnp.stack([shard_sums(parts_early[0], parts_early[1]), shard_sums(parts_late[0], parts_late[1])])
        proj_sum = proj_sum + jnp.stack([shard_sums(parts_early[2], parts_early[3]), shard_sums(parts_late[2], parts_late[3])])
        table_sum = table_sum + jnp.stack([table_early, table_late])
        gain_sum = gain_sum + jnp.stack([gain_early, gain_late])
        return ((qkv_sum, proj_sum, table_sum, gain_sum), (block_out, token_grad))
    initial = (jnp.zeros((2, D, 3 * HW), jnp.float32), jnp.zeros((2, D, HW), jnp.float32), jnp.zeros((2, 3, D), jnp.float32), jnp.zeros((2, 2, HD), jnp.float32))
    totals, outputs = lax.scan(clip_step, initial, (tokens, timestep, cotangent))
    factor = 1.0 / math.sqrt(CLIPS * FRAMES * SPATIAL)
    return (outputs[0], outputs[1], totals[0] * factor, totals[1] * factor, totals[2] * factor, totals[3] * factor)
```

```python
import math

import jax
import jax.numpy as jnp
from jax import lax
from jax.experimental import pallas as pl
from jax.experimental.pallas import tpu as pltpu
from jax.sharding import PartitionSpec as PS

HD = 72

MESH = pl.DeviceIdType.MESH
LA = 640
LB = 512


def place():
    dp = lax.axis_index("dp")
    seq = lax.axis_index("seq")
    return dp, seq, dp // 4, dp % 4, seq // 8, (seq // 2) % 4, seq % 2


def rs_kernel(factor, hid, qkb, pin, att, qkv_out, proj_out,
              hid_s, qkb_s, pin_s, att_s, P, RA, RB, SA, SB, RA2, RB2, U, V, W, X,
              act_send, act_recv, a_send, a_recv, b_send, b_recv,
              a2_send, a2_recv, b2_send, b2_recv, z_send, z_recv, f_send, f_recv):
    dp, seq, z_hi, x, y, zl, c = place()
    z = z_hi * 4 + zl
    sib = y * 8 + zl * 2 + (1 - c)

    def dev(d, s):
        return {"dp": d, "seq": s}

    barrier = pltpu.get_barrier_semaphore()
    peers = [dev(z_hi * 4 + (x + k) % 4, seq) for k in range(1, 4)]
    peers += [dev(dp, ((y + k) % 4) * 8 + zl * 2 + c) for k in range(1, 4)]
    peers += [dev(dp, ((y + k) % 4) * 8 + zl * 2 + 1 - c) for k in range(4)]
    for k in range(1, 8):
        zz = (z + k) % 8
        peers.append(dev((zz // 4) * 4 + x, y * 8 + (zz % 4) * 2 + c))
    for p in peers:
        pl.semaphore_signal(barrier, inc=1, device_id=p, device_id_type=MESH)
    pl.semaphore_wait(barrier, len(peers))

    def remote(src, dst, ss, rs, device):
        return pltpu.make_async_remote_copy(
            src_ref=src, dst_ref=dst, send_sem=ss, recv_sem=rs,
            device_id=device, device_id_type=MESH)

    acts = [
        remote(hid, hid_s, act_send.at[0], act_recv.at[0], dev(dp, sib)),
        remote(qkb.at[1 - c], qkb_s, act_send.at[1], act_recv.at[1], dev(dp, sib)),
        remote(pin, pin_s, act_send.at[2], act_recv.at[2], dev(dp, sib)),
        remote(att.at[1 - c], att_s, act_send.at[3], act_recv.at[3], dev(dp, sib)),
    ]
    for a in acts:
        a.start()
    for a in acts:
        a.wait()

    def tdot(lhs, rhs):
        return lax.dot_general(lhs, rhs, (((0,), (0,)), ((), ())),
                               preferred_element_type=jnp.float32)

    zero8 = jnp.zeros((8, 384), jnp.bfloat16)
    for b in range(2):
        def column_step(t, carry):
            lanes = pl.ds(pl.multiple_of(t * 384, 128), 384)
            acc = (tdot(qkb[c, b], hid[b, :, lanes]) + tdot(qkb_s[b], hid_s[b, :, lanes]))
            accp = (tdot(att[c, b], pin[b, :, lanes]) + tdot(att_s[b], pin_s[b, :, lanes]))
            for xo in range(4):
                for q in range(4):
                    if q < 3:
                        piece = acc[216 * xo + 72 * q: 216 * xo + 72 * q + 72]
                    else:
                        piece = accp[72 * xo: 72 * xo + 72]
                    P[xo, q, b, :, lanes] = jnp.concatenate(
                        [piece, jnp.zeros((8, 384), jnp.float32)], 0).astype(jnp.bfloat16)
            return carry
        lax.fori_loop(0, 3, column_step, 0)

    ca, cb = [], []
    for k in range(1, 4):
        xx = (x + k) % 4
        yy = (y + k) % 4
        ca.append(remote(P.at[xx, :, :, :, pl.ds(0, LA)], RA.at[k - 1], a_send.at[k - 1],
                         a_recv.at[k - 1], dev(z_hi * 4 + xx, seq)))
        cb.append(remote(P.at[:, yy, :, :, pl.ds(LA, LB)], RB.at[k - 1], b_send.at[k - 1],
                         b_recv.at[k - 1], dev(dp, yy * 8 + zl * 2 + c)))
    for k in range(3):
        ca[k].start()
        cb[k].start()
    f32 = jnp.float32
    for k in range(3):
        ca[k].wait()

    def sum_a(i, carry):
        q, b = i // 2, i % 2
        tot = P[x, q, b, :, 0:LA].astype(f32)
        for k in range(3):
            tot = tot + RA[k, q, b].astype(f32)
        SA[q, b] = tot.astype(jnp.bfloat16)
        return carry
    lax.fori_loop(0, 8, sum_a, 0)
    ca2, cb2 = [], []
    for k in range(1, 4):
        yy = (y + k) % 4
        ca2.append(remote(SA.at[yy], RA2.at[k - 1], a2_send.at[k - 1], a2_recv.at[k - 1],
                          dev(dp, yy * 8 + zl * 2 + c)))
        ca2[-1].start()
    for k in range(3):
        cb[k].wait()

    def sum_b(i, carry):
        xo, b = i // 2, i % 2
        tot = P[xo, y, b, :, LA:LA + LB].astype(f32)
        for k in range(3):
            tot = tot + RB[k, xo, b].astype(f32)
        SB[xo, b] = tot.astype(jnp.bfloat16)
        return carry
    lax.fori_loop(0, 8, sum_b, 0)
    for k in range(1, 4):
        xx = (x + k) % 4
        cb2.append(remote(SB.at[xx], RB2.at[k - 1], b2_send.at[k - 1], b2_recv.at[k - 1],
                          dev(z_hi * 4 + xx, seq)))
        cb2[-1].start()
    for k in range(3):
        ca2[k].wait()
        cb2[k].wait()
    for b in range(2):
        ta = SA[y, b].astype(f32)
        tb = SB[x, b].astype(f32)
        for k in range(3):
            ta = ta + RA2[k, b].astype(f32)
            tb = tb + RB2[k, b].astype(f32)
        full = jnp.concatenate([ta, tb], 1)
        for g in range(16):
            piece = full[:, 72 * g: 72 * g + 72]
            U[g % 4, g // 4, b] = jnp.concatenate(
                [piece, jnp.zeros((80, 56), f32)], 1).astype(jnp.bfloat16)

    for j in range(4):
        zz = c * 4 + j
        cz = remote(U.at[j], V.at[z], z_send.at[j], z_recv.at[z], dev(c * 4 + x, y * 8 + j * 2 + c))

        @pl.when(zz != z)
        def _(cz=cz):
            cz.start()

    @pl.when(z_hi == c)
    def _():
        V[z] = U[zl]
        for s in range(8):
            @pl.when(s != z)
            def _(s=s):
                remote(U.at[0], V.at[s], z_send.at[0], z_recv.at[s], dev(dp, seq)).wait_recv()
        for i in range(4):
            tot = V[0, i].astype(f32)
            for s in range(1, 8):
                tot = tot + V[s, i].astype(f32)
            W[i] = tot.astype(jnp.bfloat16)
        for yy in range(4):
            for cc in range(2):
                mine = jnp.logical_and(yy == y, cc == c)

                @pl.when(jnp.logical_not(mine))
                def _(yy=yy, cc=cc):
                    remote(W.at[yy], X.at[y], f_send.at[yy * 2 + cc], f_recv.at[y],
                           dev(dp, yy * 8 + zl * 2 + cc)).start()

                @pl.when(mine)
                def _(yy=yy):
                    X[y] = W[yy]
    for q in range(4):
        @pl.when(jnp.logical_not(jnp.logical_and(q == y, c == z_hi)))
        def _(q=q):
            remote(W.at[0], X.at[q], f_send.at[0], f_recv.at[q], dev(dp, seq)).wait_recv()

    for b in range(2):
        stacked = jnp.concatenate([X[q, b, 0:72, :].astype(f32) for q in range(4)], 0)
        turned = jnp.transpose(stacked, (1, 0)) * factor
        own = jnp.where(c == 0, turned[0:36], turned[36:72])
        qkv_out[b] = own[:, 0:216]
        proj_out[b] = own[:, 216:288]

    for j in range(4):
        zz = c * 4 + j

        @pl.when(zz != z)
        def _(j=j):
            remote(U.at[j], V.at[0], z_send.at[j], z_recv.at[0], dev(dp, seq)).wait_send()

    @pl.when(z_hi == c)
    def _():
        for yy in range(4):
            for cc in range(2):
                @pl.when(jnp.logical_not(jnp.logical_and(yy == y, cc == c)))
                def _(yy=yy, cc=cc):
                    remote(W.at[yy], X.at[0], f_send.at[yy * 2 + cc], f_recv.at[0],
                           dev(dp, seq)).wait_send()


def weight_sums(hid, qkb, pin, att, factor):
    bf = jnp.bfloat16
    dma = pltpu.SemaphoreType.DMA
    vm = pltpu.VMEM
    return pl.pallas_call(
        lambda *refs: rs_kernel(factor, *refs),
        out_shape=(jax.ShapeDtypeStruct((2, 36, 216), jnp.float32),
                   jax.ShapeDtypeStruct((2, 36, 72), jnp.float32)),
        in_specs=[pl.BlockSpec(memory_space=pltpu.VMEM)] * 4,
        out_specs=(pl.BlockSpec(memory_space=pltpu.VMEM),) * 2,
        scratch_shapes=[
            vm((2, 288, 1152), bf), vm((2, 288, 864), bf), vm((2, 288, 1152), bf), vm((2, 288, 288), bf),
            vm((4, 4, 2, 80, 1152), bf),
            vm((3, 4, 2, 80, LA), bf), vm((3, 4, 2, 80, LB), bf),
            vm((4, 2, 80, LA), bf), vm((4, 2, 80, LB), bf),
            vm((3, 2, 80, LA), bf), vm((3, 2, 80, LB), bf),
            vm((4, 4, 2, 80, 128), bf), vm((8, 4, 2, 80, 128), bf),
            vm((4, 2, 80, 128), bf), vm((4, 2, 80, 128), bf),
            dma((4,)), dma((4,)), dma((3,)), dma((3,)), dma((3,)), dma((3,)),
            dma((3,)), dma((3,)), dma((3,)), dma((3,)), dma((4,)), dma((8,)), dma((8,)), dma((4,)),
        ],
        compiler_params=pltpu.CompilerParams(
            collective_id=0, has_side_effects=True, vmem_limit_bytes=56 * 1024 * 1024),
        name="weight_sums",
    )(hid, qkb, pin, att)


def halves(qkv_back, attended):
    return (jnp.stack([qkv_back[..., :864], qkv_back[..., 864:]]),
            jnp.stack([attended[..., :288], attended[..., 288:]]))


EPSILON = 1e-06


def round_half(values):
    return values.astype(jnp.bfloat16)


def product(form, former, latter):
    return jnp.einsum(form, former, latter, preferred_element_type=jnp.float32)


def contract(former, latter):
    return lax.dot_general(
        former, latter, (((0, 1), (0, 1)), ((), ())), preferred_element_type=jnp.float32
    )


def rope_tables(length, depth):
    halfway = depth // 2
    counter = jnp.arange(halfway, dtype=jnp.float32)
    frequency = jnp.power(jnp.float32(10000.0), -2.0 * counter / depth)
    angles = jnp.arange(length, dtype=jnp.float32)[:, None] * frequency[None, :]
    return (jnp.cos(angles), jnp.sin(angles))


def rotate(vectors, rope_pair, orient):
    cosine = rope_pair[0][None, :, None, :]
    sine = orient * rope_pair[1][None, :, None, :]
    halfway = vectors.shape[-1] // 2
    leading = vectors[..., :halfway]
    trailing = vectors[..., halfway:]
    return jnp.concatenate(
        [leading * cosine - trailing * sine, trailing * cosine + leading * sine], -1
    )


def head_norm(raw_heads, gain_vec):
    widened = raw_heads.astype(jnp.float32)
    factor = lax.rsqrt(jnp.mean(widened * widened, -1, keepdims=True) + EPSILON)
    unit_vec = widened * factor
    return (unit_vec, factor, unit_vec * gain_vec)


def unit_back(unit_grad, unit_vec, factor):
    return factor * (unit_grad - unit_vec * jnp.mean(unit_grad * unit_vec, -1, keepdims=True))


def layer_forward(tokens_in, modulation, gain_pair, qkv_matrix, proj_matrix, rope_pair):
    groups, length, features = tokens_in.shape
    head_width = proj_matrix.shape[1]
    head_count = head_width // HD
    widened = tokens_in.astype(jnp.float32)
    center = widened - jnp.mean(widened, -1, keepdims=True)
    inverse = lax.rsqrt(jnp.mean(center * center, -1, keepdims=True) + EPSILON)
    normed = center * inverse
    hidden = round_half(normed * (1.0 + modulation[1]) + modulation[0])
    qkv_half = round_half(jnp.dot(hidden, qkv_matrix, preferred_element_type=jnp.float32))
    parted = qkv_half.reshape(groups, length, 3, head_count, HD)
    query_unit, query_factor, query_rot = head_norm(parted[:, :, 0], gain_pair[0])
    key_unit, key_factor, key_rot = head_norm(parted[:, :, 1], gain_pair[1])
    if rope_pair is not None:
        query_rot = rotate(query_rot, rope_pair, 1.0)
        key_rot = rotate(key_rot, rope_pair, 1.0)
    query_half = round_half(query_rot)
    key_half = round_half(key_rot)
    scores = product("glhd,gmhd->ghlm", query_half, key_half) * (1.0 / math.sqrt(HD))
    exponent = jnp.exp(scores)
    attention = exponent / jnp.sum(exponent, -1, keepdims=True)
    attention_half = round_half(attention)
    attended = round_half(product("ghlm,gmhd->glhd", attention_half, parted[:, :, 2]))
    attended = attended.reshape(groups, length, head_width)
    projected = lax.dot_general(
        attended, proj_matrix, (((2,), (1,)), ((), ())), preferred_element_type=jnp.float32
    )
    output = (widened + modulation[2] * projected).astype(jnp.bfloat16)
    stored = (
        normed,
        inverse,
        hidden,
        qkv_half,
        query_unit,
        query_factor,
        key_unit,
        key_factor,
        query_half,
        key_half,
        attention,
        attended,
        projected,
    )
    return (output, stored)


def layer_backward(grad_out, stored, modulation, gain_pair, qkv_matrix, proj_matrix, rope_pair):
    (
        normed,
        inverse,
        hidden,
        qkv_half,
        query_unit,
        query_factor,
        key_unit,
        key_factor,
        query_half,
        key_half,
        attention,
        attended,
        projected,
    ) = stored
    groups, length, features = grad_out.shape
    head_width = proj_matrix.shape[1]
    head_count = head_width // HD
    upstream = grad_out.astype(jnp.float32)
    gate_grad = jnp.sum(upstream * projected, (0, 1))
    proj_in = round_half(upstream * modulation[2])
    attended_grad = round_half(jnp.dot(proj_in, proj_matrix, preferred_element_type=jnp.float32))
    attended_grad = attended_grad.reshape(groups, length, head_count, HD)
    values = qkv_half.reshape(groups, length, 3, head_count, HD)[:, :, 2]
    attention_half = round_half(attention)
    softmax_grad = product("glhd,gmhd->ghlm", attended_grad, values)
    value_grad = product("ghlm,glhd->gmhd", attention_half, attended_grad)
    score_grad = round_half(
        attention * (softmax_grad - jnp.sum(softmax_grad * attention, -1, keepdims=True))
    )
    query_grad = product("ghlm,gmhd->glhd", score_grad, key_half) * (1.0 / math.sqrt(HD))
    key_grad = product("ghlm,glhd->gmhd", score_grad, query_half) * (1.0 / math.sqrt(HD))
    if rope_pair is not None:
        query_grad = rotate(query_grad, rope_pair, -1.0)
        key_grad = rotate(key_grad, rope_pair, -1.0)
    query_gain = jnp.sum(query_grad * query_unit, (0, 1, 2))
    key_gain = jnp.sum(key_grad * key_unit, (0, 1, 2))
    query_back = unit_back(query_grad * gain_pair[0], query_unit, query_factor)
    key_back = unit_back(key_grad * gain_pair[1], key_unit, key_factor)
    qkv_back = round_half(
        jnp.stack([query_back, key_back, value_grad], 2).reshape(groups, length, 3 * head_width)
    )
    hidden_grad = lax.dot_general(
        qkv_back, qkv_matrix, (((2,), (1,)), ((), ())), preferred_element_type=jnp.float32
    )
    shift_grad = jnp.sum(hidden_grad, (0, 1))
    scale_grad = jnp.sum(hidden_grad * normed, (0, 1))
    normed_grad = hidden_grad * (1.0 + modulation[1])
    input_grad = upstream + inverse * (
        normed_grad
        - jnp.mean(normed_grad, -1, keepdims=True)
        - normed * jnp.mean(normed_grad * normed, -1, keepdims=True)
    )
    table_terms = jnp.stack([shift_grad, scale_grad, gate_grad])
    gain_terms = jnp.stack([query_gain, key_gain])
    return (
        input_grad.astype(jnp.bfloat16),
        table_terms,
        gain_terms,
        (hidden, qkv_back, proj_in, attended),
    )


def local(tokens, timestep, time_table, block_tables, qk_gains, qkv_weight, proj_weight, cotangent):
    seq_count = lax.axis_size("seq")
    group_count = lax.axis_size("dp")
    local_tokens = tokens[0]
    frame_dev, spatial, features = local_tokens.shape
    pos_dev = spatial // seq_count
    frames = frame_dev * seq_count
    chosen = (lax.iota(jnp.int32, time_table.shape[0]) == timestep[0]).astype(jnp.float32)
    time_row = jnp.sum(chosen[:, None, None] * time_table, 0)
    modulation = block_tables + time_row[None]
    rope_pair = rope_tables(frames, HD)
    middle, spatial_stored = layer_forward(
        local_tokens, modulation[0], qk_gains[0], qkv_weight[0], proj_weight[0], None
    )
    arranged = jnp.transpose(middle, (1, 0, 2)).reshape(seq_count, pos_dev, frame_dev, features)

    def temporal_items(piece):
        output, stored = layer_forward(
            piece[0], modulation[1], qk_gains[1], qkv_weight[1], proj_weight[1], rope_pair
        )
        return (output[None],) + tuple((entry[None] for entry in stored))

    results = temporal_items(
        lax.all_to_all(arranged, "seq", split_axis=0, concat_axis=2, tiled=True)
    )
    block_out = results[0]
    temporal_stored = tuple((entry[0] for entry in results[1:]))
    middle_grad, table_late, gain_late, parts_late = layer_backward(
        cotangent[0],
        temporal_stored,
        modulation[1],
        qk_gains[1],
        qkv_weight[1],
        proj_weight[1],
        rope_pair,
    )
    returned = lax.all_to_all(
        middle_grad.reshape(pos_dev, seq_count, frame_dev, features),
        "seq",
        split_axis=1,
        concat_axis=0,
        tiled=True,
    )
    back_in = jnp.transpose(returned.reshape(spatial, frame_dev, features), (1, 0, 2))
    token_grad, table_early, gain_early, parts_early = layer_backward(
        back_in, spatial_stored, modulation[0], qk_gains[0], qkv_weight[0], proj_weight[0], None
    )
    factor = 1.0 / math.sqrt(group_count * seq_count * frame_dev * spatial)
    flat = [
        jnp.stack([early.reshape(288, -1), late.reshape(288, -1)])
        for early, late in zip(parts_early, parts_late)
    ]
    qkb, att = halves(flat[1], flat[3])
    qkv_grad, proj_grad = weight_sums(flat[0], qkb, flat[2], att, factor)
    table_grad, gain_grad = lax.psum(
        (jnp.stack([table_early, table_late]), jnp.stack([gain_early, gain_late])), ("dp", "seq")
    )
    return (
        block_out,
        token_grad[None],
        qkv_grad,
        proj_grad,
        table_grad * factor,
        gain_grad * factor,
    )


def solution(mesh):
    return jax.shard_map(
        local,
        mesh=mesh,
        in_specs=(
            PS("dp", "seq", None, None),
            PS("dp"),
            PS(),
            PS(),
            PS(),
            PS(),
            PS(),
            PS("dp", "seq", None, None),
        ),
        out_specs=(
            PS("dp", "seq", None, None),
            PS("dp", "seq", None, None),
            PS(None, "seq", "dp"),
            PS(None, "seq", "dp"),
            PS(),
            PS(),
        ),
        check_vma=False,
    )
```

```python
import math

import numpy as np
import jax
import jax.numpy as jnp
from jax import lax
from jax.experimental import pallas as pl
from jax.experimental.pallas import tpu as pltpu
from jax.sharding import PartitionSpec as PS

MESH = pl.DeviceIdType.MESH

HD = 72
EPS = 1e-06
F32 = jnp.float32
BF = jnp.bfloat16
SCALE = 1.0 / math.sqrt(HD)


def mm(a, b):
    return lax.dot_general(a, b, (((1,), (0,)), ((), ())), preferred_element_type=F32)


def mm_nt(a, b):
    return lax.dot_general(a, b, (((1,), (1,)), ((), ())), preferred_element_type=F32)


def mm_tn(a, b):
    return lax.dot_general(a, b, (((0,), (0,)), ((), ())), preferred_element_type=F32)


def row_norm(u):
    center = u - jnp.mean(u, -1, keepdims=True)
    inverse = lax.rsqrt(jnp.mean(center * center, -1, keepdims=True) + EPS)
    return center * inverse, inverse


def swap(x):
    return jnp.concatenate([x[:, 36:72], x[:, 0:36]], 1)


def spin(x, rope, sign):
    if rope is None:
        return x
    cosine, sine = rope
    return x * cosine + sign * (swap(x) * sine)


def unit_of(raw):
    wide = raw.astype(F32)
    factor = lax.rsqrt(jnp.mean(wide * wide, -1, keepdims=True) + EPS)
    return wide * factor, factor


def unit_back(grad, unit, factor):
    return factor * (grad - unit * jnp.mean(grad * unit, -1, keepdims=True))


def softmax(qh, kh):
    e = jnp.exp(mm_nt(qh, kh) * SCALE)
    return e / jnp.sum(e, -1, keepdims=True)


def heads_of(qkv, h, gain, rope):
    qu, qf = unit_of(qkv[:, 72 * h: 72 * h + 72])
    ku, kf = unit_of(qkv[:, 576 + 72 * h: 576 + 72 * h + 72])
    v = qkv[:, 1152 + 72 * h: 1152 + 72 * h + 72]
    qh = spin(qu * gain[0:1], rope, 1.0).astype(BF)
    kh = spin(ku * gain[1:2], rope, 1.0).astype(BF)
    return qu, qf, ku, kf, qh, kh, v


def modulation(block, ts_ref, time_ref, table_ref, mod_ref):
    mod_ref[...] = table_ref[:, block] + time_ref[:, pl.ds(ts_ref[0], 1), :].reshape(3, 1152)


def load_weights(block, w_hbm, wp_hbm, w_ref, wp_ref, sem):
    copies = [pltpu.make_async_copy(w_hbm.at[block], w_ref, sem.at[0]),
              pltpu.make_async_copy(wp_hbm.at[block], wp_ref, sem.at[1])]
    for copy in copies:
        copy.start()
    return copies


def forward_kernel(ts_ref, time_ref, table_ref, gains_ref, w_hbm, wp_hbm, u_ref,
                   out_ref, qkv_ref, att_ref, mod_ref, w_ref, wp_ref, sem):
    loads = load_weights(0, w_hbm, wp_hbm, w_ref, wp_ref, sem)
    modulation(0, ts_ref, time_ref, table_ref, mod_ref)
    gain_ref = gains_ref.at[0]
    u = u_ref[...].astype(F32)
    normed, _ = row_norm(u)
    hidden = (normed * (1.0 + mod_ref[1:2]) + mod_ref[0:1]).astype(BF)
    loads[0].wait()
    qkv_ref[...] = mm_nt(hidden, w_ref[...]).astype(BF)
    gain = gain_ref[...]
    parts = []
    for h in range(8):
        _, _, _, _, qh, kh, v = heads_of(qkv_ref, h, gain, None)
        rows = []
        for g in range(3):
            s = slice(96 * g, 96 * g + 96)
            rows.append(mm(softmax(qh[s], kh[s]).astype(BF), v[s]))
        parts.append(jnp.concatenate(rows, 0).astype(BF))
    att_ref[...] = jnp.concatenate(parts, 1)
    loads[1].wait()
    out_ref[...] = (u + mod_ref[2:3] * mm(att_ref[...], wp_ref[...])).astype(BF)


def backward_body(forward, loads, u_ref, g_ref, mod_ref, gain_ref, w_ref, wp_ref, rope, qkv_ref, att_ref,
                  out_ref, grad_ref, hid_ref, qkb_ref, pin_ref, atth_ref, stat_ref, dat_ref):
    scale1 = 1.0 + mod_ref[1:2]
    gate = mod_ref[2:3]
    u = u_ref[...].astype(F32)
    normed, inverse = row_norm(u)
    hid_ref[...] = (normed * scale1 + mod_ref[0:1]).astype(BF)
    loads[0].wait()
    if forward:
        qkv_ref[...] = mm_nt(hid_ref[...], w_ref[...]).astype(BF)
    pin_ref[...] = (g_ref[...].astype(F32) * gate).astype(BF)
    loads[1].wait()
    dat_ref[...] = mm_nt(pin_ref[...], wp_ref[...]).astype(BF)
    gain = gain_ref[...]
    att_parts, back_q, back_k, back_v = [], [], [], []
    gq = jnp.zeros((1, 72), F32)
    gk = jnp.zeros((1, 72), F32)
    for h in range(8):
        qu, qf, ku, kf, qh, kh, v = heads_of(qkv_ref, h, gain, rope)
        da = dat_ref[:, 72 * h: 72 * h + 72]
        avs, dqs, dks, dvs = [], [], [], []
        for g in range(3):
            s = slice(96 * g, 96 * g + 96)
            att = softmax(qh[s], kh[s])
            att16 = att.astype(BF)
            if forward:
                avs.append(mm(att16, v[s]))
            dp = mm_nt(da[s], v[s])
            dvs.append(mm_tn(att16, da[s]))
            ds = (att * (dp - jnp.sum(dp * att, -1, keepdims=True))).astype(BF)
            dqs.append(mm(ds, kh[s]) * SCALE)
            dks.append(mm_tn(ds, qh[s]) * SCALE)
        if forward:
            att_parts.append(jnp.concatenate(avs, 0).astype(BF))
        dq = spin(jnp.concatenate(dqs, 0), rope, -1.0)
        dk = spin(jnp.concatenate(dks, 0), rope, -1.0)
        gq = gq + jnp.sum(dq * qu, 0, keepdims=True)
        gk = gk + jnp.sum(dk * ku, 0, keepdims=True)
        back_q.append(unit_back(dq * gain[0:1], qu, qf).astype(BF))
        back_k.append(unit_back(dk * gain[1:2], ku, kf).astype(BF))
        back_v.append(jnp.concatenate(dvs, 0).astype(BF))
    qkv_back = jnp.concatenate(back_q + back_k + back_v, 1)
    qkb_ref[0] = qkv_back[:, 0:864]
    qkb_ref[1] = qkv_back[:, 864:1728]
    if forward:
        att_ref[...] = jnp.concatenate(att_parts, 1)
    attended = att_ref[...]
    atth_ref[0] = attended[:, 0:288]
    atth_ref[1] = attended[:, 288:576]
    projected = mm(attended, wp_ref[...])
    if forward:
        out_ref[...] = (u_ref[...].astype(F32) + gate * projected).astype(BF)
    up = g_ref[...].astype(F32)
    hg = mm(qkv_back, w_ref[...])
    normed, inverse = row_norm(u_ref[...].astype(F32))
    stat_ref[...] = jnp.concatenate([
        jnp.sum(hg, 0, keepdims=True),
        jnp.sum(hg * normed, 0, keepdims=True),
        jnp.sum(up * projected, 0, keepdims=True),
        jnp.concatenate([gq, jnp.zeros((1, 56), F32), gk, jnp.zeros((1, 1152 - 200), F32)], 1),
        jnp.zeros((4, 1152), F32)], 0)
    ng = hg * scale1
    grad_ref[...] = (up + inverse * (
        ng - jnp.mean(ng, -1, keepdims=True)
        - normed * jnp.mean(ng * normed, -1, keepdims=True))).astype(BF)


def temporal_kernel(ts_ref, time_ref, table_ref, gains_ref, w_hbm, wp_hbm, u_ref, g_ref, cos_ref, sin_ref,
                    out_ref, grad_ref, hid_ref, qkb_ref, pin_ref, atth_ref, stat_ref,
                    qkv_ref, att_ref, dat_ref, mod_ref, w_ref, wp_ref, sem):
    loads = load_weights(1, w_hbm, wp_hbm, w_ref, wp_ref, sem)
    modulation(1, ts_ref, time_ref, table_ref, mod_ref)
    backward_body(True, loads, u_ref, g_ref, mod_ref, gains_ref.at[1], w_ref, wp_ref,
                  (cos_ref[...], sin_ref[...]), qkv_ref, att_ref,
                  out_ref, grad_ref, hid_ref, qkb_ref, pin_ref, atth_ref, stat_ref, dat_ref)


def spatial_back_kernel(ts_ref, time_ref, table_ref, gains_ref, w_hbm, wp_hbm, u_ref, g_ref, qkv_ref, att_ref,
                        grad_ref, hid_ref, qkb_ref, pin_ref, atth_ref, stat_ref,
                        dat_ref, mod_ref, w_ref, wp_ref, sem):
    loads = load_weights(0, w_hbm, wp_hbm, w_ref, wp_ref, sem)
    modulation(0, ts_ref, time_ref, table_ref, mod_ref)
    backward_body(False, loads, u_ref, g_ref, mod_ref, gains_ref.at[0], w_ref, wp_ref, None, qkv_ref, att_ref,
                  None, grad_ref, hid_ref, qkb_ref, pin_ref, atth_ref, stat_ref, dat_ref)


VM = pl.BlockSpec(memory_space=pltpu.VMEM)
HBM = pl.BlockSpec(memory_space=pl.ANY)
SMEM = pl.BlockSpec(memory_space=pltpu.SMEM)
PARAM_SPECS = [SMEM, VM, VM, VM, HBM, HBM]
LIMIT = 56 * 1024 * 1024
WEIGHT_SCRATCH = [pltpu.VMEM((3, 1152), F32), pltpu.VMEM((1728, 1152), BF),
                  pltpu.VMEM((576, 1152), BF), pltpu.SemaphoreType.DMA((2,))]


def sds(shape, dtype=BF):
    return jax.ShapeDtypeStruct(shape, dtype)


def call(kernel, outs, params, arrays, scratch, name):
    return pl.pallas_call(
        kernel, out_shape=outs, in_specs=PARAM_SPECS + [VM] * len(arrays), out_specs=(VM,) * len(outs),
        scratch_shapes=scratch + WEIGHT_SCRATCH,
        compiler_params=pltpu.CompilerParams(vmem_limit_bytes=LIMIT), name=name,
    )(*params, *arrays)


BACK_OUT = (sds((288, 1152)), sds((288, 1152)), sds((2, 288, 864)), sds((288, 1152)),
            sds((2, 288, 288)), sds((8, 1152), F32))


def rope_arrays():
    freq = np.power(10000.0, -2.0 * np.arange(36) / HD)
    angle = np.arange(96)[:, None] * freq[None]
    cosine = np.concatenate([np.cos(angle)] * 2, 1)
    sine = np.concatenate([-np.sin(angle), np.sin(angle)], 1)
    return (jnp.asarray(np.tile(cosine, (3, 1)), F32), jnp.asarray(np.tile(sine, (3, 1)), F32))


def spatial_forward(params, u):
    return call(forward_kernel, (sds((288, 1152)), sds((288, 1728)), sds((288, 576))), params, (u,), [],
                "spatial_forward")


def temporal(params, u, g):
    half = pltpu.VMEM((288, 576), BF)
    return call(temporal_kernel, (sds((288, 1152)),) + BACK_OUT, params, (u, g) + rope_arrays(),
                [pltpu.VMEM((288, 1728), BF), half, half], "temporal")


def spatial_back(params, u, g, qkv, att):
    return call(spatial_back_kernel, BACK_OUT, params, (u, g, qkv, att), [pltpu.VMEM((288, 576), BF)],
                "spatial_back")


def selector(rows, columns, place):
    at = lax.broadcasted_iota(jnp.int32, (rows, columns), 0)
    return jnp.where(lax.broadcasted_iota(jnp.int32, (rows, columns), 1) == place(at), 1.0, 0.0).astype(BF)


def pack(value, out_ref, count):
    def at(r, j):
        a = (r * 11) >> 5
        return 96 * a + 3 * j + r - 3 * a

    def first(i):
        r = i & 15
        return jnp.where(r < 9, at(r, i >> 4), -1)

    def second(i):
        r = i & 15
        return jnp.where(r >= 9, at(r - 9, i >> 4), -1)

    def third(i):
        r = i & 15
        return jnp.where(jnp.logical_or(r == 9, r == 10), at(r - 2, i >> 4), -1)
    s1 = selector(512, 288, first)
    tail = value[:, 768:1152]
    low = mm(s1, value[:, 0:384]) + mm(selector(512, 288, second), tail)
    high = mm(s1, value[:, 384:768]) + mm(selector(512, 288, third), tail)
    out_ref[:, :, 0:384] = low.astype(BF).reshape(32, 16, 384)
    out_ref[:, :, 384:768] = high.astype(BF).reshape(32, 16, 384)


def unpack(parcel_ref):
    def source(o):
        b = (o >= 96).astype(jnp.int32) + (o >= 192).astype(jnp.int32)
        rest = o - 96 * b
        i = (rest * 683) >> 11
        return 16 * i, 3 * (rest - 3 * i) + b

    def first(o):
        base, r = source(o)
        return base + r

    def second(o):
        base, r = source(o)
        return jnp.where(r < 7, base + 9 + r, -1)

    def third(o):
        base, r = source(o)
        return jnp.where(r >= 7, base + 2 + r, -1)
    low = parcel_ref[:, :, 0:384].reshape(512, 384)
    high = parcel_ref[:, :, 384:768].reshape(512, 384)
    t1 = selector(288, 512, first)
    tail = mm(selector(288, 512, second), low) + mm(selector(288, 512, third), high)
    return jnp.concatenate([mm(t1, low), mm(t1, high), tail], 1).astype(BF)


def exchange_kernel(u_ref, out_ref, parcel, landed, send, recv):
    dp = lax.axis_index("dp")
    seq = lax.axis_index("seq")
    barrier = pltpu.get_barrier_semaphore()
    for k in range(1, 32):
        pl.semaphore_signal(barrier, inc=1, device_id={"dp": dp, "seq": (seq + k) % 32}, device_id_type=MESH)
    pack(u_ref[...], parcel, 32)
    pl.semaphore_wait(barrier, 31)
    copies = []
    for k in range(1, 32):
        to = (seq + k) % 32
        copies.append(pltpu.make_async_remote_copy(
            src_ref=parcel.at[to], dst_ref=landed.at[seq], send_sem=send.at[k], recv_sem=recv.at[k],
            device_id={"dp": dp, "seq": to}, device_id_type=MESH))
    for copy in copies:
        copy.start()
    landed[seq] = parcel[seq]
    for copy in copies:
        copy.wait()
    out_ref[...] = unpack(landed)


def exchange(u, collective_id):
    return pl.pallas_call(
        exchange_kernel, out_shape=sds((288, 1152)), in_specs=[VM], out_specs=VM,
        scratch_shapes=[pltpu.VMEM((32, 16, 768), BF), pltpu.VMEM((32, 16, 768), BF),
                        pltpu.SemaphoreType.DMA((32,)), pltpu.SemaphoreType.DMA((32,))],
        compiler_params=pltpu.CompilerParams(collective_id=collective_id, has_side_effects=True,
                                             vmem_limit_bytes=LIMIT),
        name="exchange",
    )(u)


LA = 640
LB = 512


def place():
    dp = lax.axis_index("dp")
    seq = lax.axis_index("seq")
    return dp, seq, dp // 4, dp % 4, seq // 8, (seq // 2) % 4, seq % 2


def rs_kernel(factor, hid0, qkb0, pin0, att0, stat0, hid1, qkb1, pin1, att1, stat1,
              qkv_out, proj_out, table_out, gain_out, hid_s, qkb_s, pin_s, att_s, P, RA, RB, SA, SB, RA2, RB2, U, V, W, X,
              act_send, act_recv, a_send, a_recv, b_send, b_recv,
              a2_send, a2_recv, b2_send, b2_recv, z_send, z_recv, f_send, f_recv,
              T, TC, TX, TY, TZ, t_send, t_recv):
    hid, qkb, pin, att = (hid0, hid1), (qkb0, qkb1), (pin0, pin1), (att0, att1)
    dp, seq, z_hi, x, y, zl, c = place()
    z = z_hi * 4 + zl
    sib = y * 8 + zl * 2 + (1 - c)

    def dev(d, s):
        return {"dp": d, "seq": s}

    barrier = pltpu.get_barrier_semaphore()
    peers = [dev(z_hi * 4 + (x + k) % 4, seq) for k in range(1, 4)]
    peers += [dev(dp, ((y + k) % 4) * 8 + zl * 2 + c) for k in range(1, 4)]
    peers += [dev(dp, ((y + k) % 4) * 8 + zl * 2 + 1 - c) for k in range(4)]
    for k in range(1, 8):
        zz = (z + k) % 8
        peers.append(dev((zz // 4) * 4 + x, y * 8 + (zz % 4) * 2 + c))
    for p in peers:
        pl.semaphore_signal(barrier, inc=1, device_id=p, device_id_type=MESH)
    pl.semaphore_wait(barrier, len(peers))

    def remote(src, dst, ss, rs, device):
        return pltpu.make_async_remote_copy(
            src_ref=src, dst_ref=dst, send_sem=ss, recv_sem=rs,
            device_id=device, device_id_type=MESH)

    def stat_start(level, slots, me, targets):
        slots[me] = T[...]
        copies = [remote(T, slots.at[me], t_send.at[level, k], t_recv.at[level, k], target)
                  for k, target in enumerate(targets)]
        for copy in copies:
            copy.start()
        return copies

    def stat_end(copies, slots, count):
        for copy in copies:
            copy.wait()
        total = slots[0]
        for k in range(1, count):
            total = total + slots[k]
        T[...] = total

    T[...] = jnp.concatenate([stat0[0:3], stat1[0:3], stat0[3:4], stat1[3:4]], 0)
    stats = stat_start(0, TC, c, [dev(dp, sib)])
    acts = []
    for b in range(2):
        for i, (src, dst) in enumerate(((hid[b], hid_s.at[b]), (qkb[b].at[1 - c], qkb_s.at[b]),
                                        (pin[b], pin_s.at[b]), (att[b].at[1 - c], att_s.at[b]))):
            acts.append(remote(src, dst, act_send.at[b, i], act_recv.at[b, i], dev(dp, sib)))
            acts[-1].start()
    for a in acts:
        a.wait()
    stat_end(stats, TC, 2)
    stats = stat_start(1, TX, x, [dev(z_hi * 4 + (x + k) % 4, seq) for k in range(1, 4)])

    def tdot(lhs, rhs):
        return lax.dot_general(lhs, rhs, (((0,), (0,)), ((), ())),
                               preferred_element_type=jnp.float32)

    zero8 = jnp.zeros((8, 384), jnp.bfloat16)
    for b in range(2):
        def column_step(t, carry):
            lanes = pl.ds(pl.multiple_of(t * 384, 128), 384)
            acc = (tdot(qkb[b][c], hid[b][:, lanes]) + tdot(qkb_s[b], hid_s[b, :, lanes]))
            accp = (tdot(att[b][c], pin[b][:, lanes]) + tdot(att_s[b], pin_s[b, :, lanes]))
            for xo in range(4):
                for q in range(4):
                    if q < 3:
                        piece = acc[216 * xo + 72 * q: 216 * xo + 72 * q + 72]
                    else:
                        piece = accp[72 * xo: 72 * xo + 72]
                    P[xo, q, b, :, lanes] = jnp.concatenate(
                        [piece, jnp.zeros((8, 384), jnp.float32)], 0).astype(jnp.bfloat16)
            return carry
        lax.fori_loop(0, 3, column_step, 0)

    ca, cb = [], []
    for k in range(1, 4):
        xx = (x + k) % 4
        yy = (y + k) % 4
        ca.append(remote(P.at[xx, :, :, :, pl.ds(0, LA)], RA.at[k - 1], a_send.at[k - 1],
                         a_recv.at[k - 1], dev(z_hi * 4 + xx, seq)))
        cb.append(remote(P.at[:, yy, :, :, pl.ds(LA, LB)], RB.at[k - 1], b_send.at[k - 1],
                         b_recv.at[k - 1], dev(dp, yy * 8 + zl * 2 + c)))
    for k in range(3):
        ca[k].start()
        cb[k].start()
    f32 = jnp.float32
    stat_end(stats, TX, 4)
    stats = stat_start(2, TY, y, [dev(dp, ((y + k) % 4) * 8 + zl * 2 + c) for k in range(1, 4)])
    for k in range(3):
        ca[k].wait()

    def sum_a(i, carry):
        q, b = i // 2, i % 2
        tot = P[x, q, b, :, 0:LA].astype(f32)
        for k in range(3):
            tot = tot + RA[k, q, b].astype(f32)
        SA[q, b] = tot.astype(jnp.bfloat16)
        return carry
    lax.fori_loop(0, 8, sum_a, 0)
    ca2, cb2 = [], []
    for k in range(1, 4):
        yy = (y + k) % 4
        ca2.append(remote(SA.at[yy], RA2.at[k - 1], a2_send.at[k - 1], a2_recv.at[k - 1],
                          dev(dp, yy * 8 + zl * 2 + c)))
        ca2[-1].start()
    for k in range(3):
        cb[k].wait()

    def sum_b(i, carry):
        xo, b = i // 2, i % 2
        tot = P[xo, y, b, :, LA:LA + LB].astype(f32)
        for k in range(3):
            tot = tot + RB[k, xo, b].astype(f32)
        SB[xo, b] = tot.astype(jnp.bfloat16)
        return carry
    lax.fori_loop(0, 8, sum_b, 0)
    for k in range(1, 4):
        xx = (x + k) % 4
        cb2.append(remote(SB.at[xx], RB2.at[k - 1], b2_send.at[k - 1], b2_recv.at[k - 1],
                          dev(z_hi * 4 + xx, seq)))
        cb2[-1].start()
    stat_end(stats, TY, 4)
    stats = stat_start(3, TZ, z, [dev((((z + k) % 8) // 4) * 4 + x, y * 8 + ((z + k) % 4) * 2 + c)
                                  for k in range(1, 8)])
    for k in range(3):
        ca2[k].wait()
        cb2[k].wait()
    for b in range(2):
        ta = SA[y, b].astype(f32)
        tb = SB[x, b].astype(f32)
        for k in range(3):
            ta = ta + RA2[k, b].astype(f32)
            tb = tb + RB2[k, b].astype(f32)
        full = jnp.concatenate([ta, tb], 1)
        for g in range(16):
            piece = full[:, 72 * g: 72 * g + 72]
            U[g % 4, g // 4, b] = jnp.concatenate(
                [piece, jnp.zeros((80, 56), f32)], 1).astype(jnp.bfloat16)

    for j in range(4):
        zz = c * 4 + j
        cz = remote(U.at[j], V.at[z], z_send.at[j], z_recv.at[z], dev(c * 4 + x, y * 8 + j * 2 + c))

        @pl.when(zz != z)
        def _(cz=cz):
            cz.start()

    @pl.when(z_hi == c)
    def _():
        V[z] = U[zl]
        for s in range(8):
            @pl.when(s != z)
            def _(s=s):
                remote(U.at[0], V.at[s], z_send.at[0], z_recv.at[s], dev(dp, seq)).wait_recv()
        for i in range(4):
            tot = V[0, i].astype(f32)
            for s in range(1, 8):
                tot = tot + V[s, i].astype(f32)
            W[i] = tot.astype(jnp.bfloat16)
        for yy in range(4):
            for cc in range(2):
                mine = jnp.logical_and(yy == y, cc == c)

                @pl.when(jnp.logical_not(mine))
                def _(yy=yy, cc=cc):
                    remote(W.at[yy], X.at[y], f_send.at[yy * 2 + cc], f_recv.at[y],
                           dev(dp, yy * 8 + zl * 2 + cc)).start()

                @pl.when(mine)
                def _(yy=yy):
                    X[y] = W[yy]
    for q in range(4):
        @pl.when(jnp.logical_not(jnp.logical_and(q == y, c == z_hi)))
        def _(q=q):
            remote(W.at[0], X.at[q], f_send.at[0], f_recv.at[q], dev(dp, seq)).wait_recv()

    for b in range(2):
        stacked = jnp.concatenate([X[q, b, 0:72, :].astype(f32) for q in range(4)], 0)
        turned = jnp.transpose(stacked, (1, 0)) * factor
        own = jnp.where(c == 0, turned[0:36], turned[36:72])
        qkv_out[:, b] = own[:, 0:216]
        proj_out[:, b] = own[:, 216:288]

    stat_end(stats, TZ, 8)
    total = T[...] * factor
    table_out[:, 0] = total[0:3]
    table_out[:, 1] = total[3:6]
    for b in range(2):
        gain_out[b] = jnp.concatenate([total[6 + b:7 + b, 0:72], total[6 + b:7 + b, 128:200]], 0)

    for j in range(4):
        zz = c * 4 + j

        @pl.when(zz != z)
        def _(j=j):
            remote(U.at[j], V.at[0], z_send.at[j], z_recv.at[0], dev(dp, seq)).wait_send()

    @pl.when(z_hi == c)
    def _():
        for yy in range(4):
            for cc in range(2):
                @pl.when(jnp.logical_not(jnp.logical_and(yy == y, cc == c)))
                def _(yy=yy, cc=cc):
                    remote(W.at[yy], X.at[0], f_send.at[yy * 2 + cc], f_recv.at[0],
                           dev(dp, seq)).wait_send()


def weight_sums(early, late, factor):
    dma = pltpu.SemaphoreType.DMA
    vm = pltpu.VMEM
    return pl.pallas_call(
        lambda *refs: rs_kernel(factor, *refs),
        out_shape=(sds((36, 2, 216), F32), sds((36, 2, 72), F32),
                   sds((3, 2, 1152), F32), sds((2, 2, 72), F32)),
        in_specs=[VM] * 10, out_specs=(VM,) * 4,
        scratch_shapes=[
            vm((2, 288, 1152), BF), vm((2, 288, 864), BF), vm((2, 288, 1152), BF), vm((2, 288, 288), BF),
            vm((4, 4, 2, 80, 1152), BF),
            vm((3, 4, 2, 80, LA), BF), vm((3, 4, 2, 80, LB), BF),
            vm((4, 2, 80, LA), BF), vm((4, 2, 80, LB), BF),
            vm((3, 2, 80, LA), BF), vm((3, 2, 80, LB), BF),
            vm((4, 4, 2, 80, 128), BF), vm((8, 4, 2, 80, 128), BF),
            vm((4, 2, 80, 128), BF), vm((4, 2, 80, 128), BF),
            dma((2, 4)), dma((2, 4)), dma((3,)), dma((3,)), dma((3,)), dma((3,)),
            dma((3,)), dma((3,)), dma((3,)), dma((3,)), dma((4,)), dma((8,)), dma((8,)), dma((4,)),
            vm((8, 1152), F32), vm((2, 8, 1152), F32), vm((4, 8, 1152), F32), vm((4, 8, 1152), F32),
            vm((8, 8, 1152), F32), dma((4, 7)), dma((4, 7)),
        ],
        compiler_params=pltpu.CompilerParams(
            collective_id=0, has_side_effects=True, vmem_limit_bytes=LIMIT),
        name="weight_sums",
    )(*early, *late)


def local(tokens, timestep, time_table, block_tables, qk_gains, qkv_weight, proj_weight, cotangent):
    frame_dev, spatial, features = tokens.shape[1:]
    shape = (1, frame_dev, spatial, features)
    count = lax.axis_size("dp") * lax.axis_size("seq") * frame_dev * spatial
    params = (timestep, jnp.swapaxes(time_table, 0, 1), jnp.swapaxes(block_tables, 0, 1), qk_gains,
              jnp.swapaxes(qkv_weight, 1, 2), jnp.swapaxes(proj_weight, 1, 2))
    u = tokens.reshape(288, 1152)
    middle, qkv, att = spatial_forward(params, u)
    block_out, middle_grad, *late = temporal(params, exchange(middle, 1), cotangent.reshape(288, 1152))
    token_grad, *early = spatial_back(params, u, exchange(middle_grad, 1), qkv, att)
    qkv_grad, proj_grad, table_grad, gain_grad = weight_sums(early, late, 1.0 / math.sqrt(count))
    return (block_out.reshape(shape), token_grad.reshape(shape), jnp.swapaxes(qkv_grad, 0, 1),
            jnp.swapaxes(proj_grad, 0, 1), jnp.swapaxes(table_grad, 0, 1), gain_grad)


def solution(mesh):
    return jax.shard_map(
        local,
        mesh=mesh,
        in_specs=(
            PS("dp", "seq", None, None),
            PS("dp"),
            PS(),
            PS(),
            PS(),
            PS(),
            PS(),
            PS("dp", "seq", None, None),
        ),
        out_specs=(
            PS("dp", "seq", None, None),
            PS("dp", "seq", None, None),
            PS(None, "seq", "dp"),
            PS(None, "seq", "dp"),
            PS(),
            PS(),
        ),
        check_vma=False,
    )
```

```python
import math

import numpy as np
import jax
import jax.numpy as jnp
from jax import lax
from jax.experimental import pallas as pl
from jax.experimental.pallas import tpu as pltpu
from jax.sharding import PartitionSpec as PS

MESH = pl.DeviceIdType.MESH

HD = 72
EPS = 1e-06
F32 = jnp.float32
BF = jnp.bfloat16
SCALE = 1.0 / math.sqrt(HD)


def mm(a, b):
    return lax.dot_general(a, b, (((1,), (0,)), ((), ())), preferred_element_type=F32)


def mm_nt(a, b):
    return lax.dot_general(a, b, (((1,), (1,)), ((), ())), preferred_element_type=F32)


def mm_tn(a, b):
    return lax.dot_general(a, b, (((0,), (0,)), ((), ())), preferred_element_type=F32)


def row_norm(u):
    center = u - jnp.mean(u, -1, keepdims=True)
    inverse = lax.rsqrt(jnp.mean(center * center, -1, keepdims=True) + EPS)
    return center * inverse, inverse


def swap(x):
    return jnp.concatenate([x[:, 36:72], x[:, 0:36]], 1)


def spin(x, rope, sign):
    if rope is None:
        return x
    cosine, sine = rope
    return x * cosine + sign * (swap(x) * sine)


def unit_of(raw):
    wide = raw.astype(F32)
    factor = lax.rsqrt(jnp.mean(wide * wide, -1, keepdims=True) + EPS)
    return wide * factor, factor


def unit_back(grad, unit, factor):
    return factor * (grad - unit * jnp.mean(grad * unit, -1, keepdims=True))


def softmax(qh, kh):
    e = jnp.exp(mm_nt(qh, kh) * SCALE)
    return e / jnp.sum(e, -1, keepdims=True)


def heads_of(qkv, h, gain, rope):
    qu, qf = unit_of(qkv[:, 72 * h: 72 * h + 72])
    ku, kf = unit_of(qkv[:, 576 + 72 * h: 576 + 72 * h + 72])
    v = qkv[:, 1152 + 72 * h: 1152 + 72 * h + 72]
    qh = spin(qu * gain[0:1], rope, 1.0).astype(BF)
    kh = spin(ku * gain[1:2], rope, 1.0).astype(BF)
    return qu, qf, ku, kf, qh, kh, v


def modulation(block, ts_ref, time_ref, table_ref, mod_ref):
    mod_ref[...] = table_ref[:, block] + time_ref[:, pl.ds(ts_ref[0], 1), :].reshape(3, 1152)


def load_weights(block, w_hbm, wp_hbm, w_ref, wp_ref, sem):
    copies = [pltpu.make_async_copy(w_hbm.at[block], w_ref, sem.at[0]),
              pltpu.make_async_copy(wp_hbm.at[block], wp_ref, sem.at[1])]
    for copy in copies:
        copy.start()
    return copies


def forward_kernel(ts_ref, time_ref, table_ref, gains_ref, w_hbm, wp_hbm, u_ref,
                   out_ref, qkv_ref, att_ref, mod_ref, _, w_ref, wp_ref, sem):
    loads = load_weights(0, w_hbm, wp_hbm, w_ref, wp_ref, sem)
    modulation(0, ts_ref, time_ref, table_ref, mod_ref)
    gain_ref = gains_ref.at[0]
    u = u_ref[...].astype(F32)
    normed, _ = row_norm(u)
    hidden = (normed * (1.0 + mod_ref[1:2]) + mod_ref[0:1]).astype(BF)
    loads[0].wait()
    qkv_ref[...] = mm_nt(hidden, w_ref[...]).astype(BF)
    gain = gain_ref[...]
    parts = []
    for h in range(8):
        _, _, _, _, qh, kh, v = heads_of(qkv_ref, h, gain, None)
        rows = []
        for g in range(3):
            s = slice(96 * g, 96 * g + 96)
            rows.append(mm(softmax(qh[s], kh[s]).astype(BF), v[s]))
        parts.append(jnp.concatenate(rows, 0).astype(BF))
    att_ref[...] = jnp.concatenate(parts, 1)
    loads[1].wait()
    out_ref[...] = (u + mod_ref[2:3] * mm(att_ref[...], wp_ref[...])).astype(BF)


def before_heads(scale1, mod_ref, u_ref, g_ref, wp_ref, hid_ref, pin_ref, dat_ref):
    normed, _ = row_norm(u_ref[...].astype(F32))
    hid_ref[...] = (normed * scale1 + mod_ref[0:1]).astype(BF)
    pin_ref[...] = (g_ref[...].astype(F32) * mod_ref[2:3]).astype(BF)
    dat_ref[...] = mm_nt(pin_ref[...], wp_ref[...]).astype(BF)


class Heads:
    def __init__(self, forward, gain, rope, qkv_ref, dat_ref):
        self.forward, self.gain, self.rope = forward, gain, rope
        self.qkv_ref, self.dat_ref = qkv_ref, dat_ref
        self.att, self.back = [], ([], [], [])
        self.gq = jnp.zeros((1, 72), F32)
        self.gk = jnp.zeros((1, 72), F32)

    def step(self, h):
        gain, rope = self.gain, self.rope
        qu, qf, ku, kf, qh, kh, v = heads_of(self.qkv_ref, h, gain, rope)
        da = self.dat_ref[:, 72 * h: 72 * h + 72]
        avs, dqs, dks, dvs = [], [], [], []
        for g in range(3):
            s = slice(96 * g, 96 * g + 96)
            att = softmax(qh[s], kh[s])
            att16 = att.astype(BF)
            if self.forward:
                avs.append(mm(att16, v[s]))
            dp = mm_nt(da[s], v[s])
            dvs.append(mm_tn(att16, da[s]))
            ds = (att * (dp - jnp.sum(dp * att, -1, keepdims=True))).astype(BF)
            dqs.append(mm(ds, kh[s]) * SCALE)
            dks.append(mm_tn(ds, qh[s]) * SCALE)
        if self.forward:
            self.att.append(jnp.concatenate(avs, 0).astype(BF))
        dq = spin(jnp.concatenate(dqs, 0), rope, -1.0)
        dk = spin(jnp.concatenate(dks, 0), rope, -1.0)
        self.gq = self.gq + jnp.sum(dq * qu, 0, keepdims=True)
        self.gk = self.gk + jnp.sum(dk * ku, 0, keepdims=True)
        self.back[0].append(unit_back(dq * gain[0:1], qu, qf).astype(BF))
        self.back[1].append(unit_back(dk * gain[1:2], ku, kf).astype(BF))
        self.back[2].append(jnp.concatenate(dvs, 0).astype(BF))

    def qkv_back(self):
        return jnp.concatenate(self.back[0] + self.back[1] + self.back[2], 1)

    def gain_row(self):
        return jnp.concatenate([self.gq, jnp.zeros((1, 56), F32), self.gk,
                                jnp.zeros((1, 1152 - 200), F32)], 1)


def after_heads(scale1, u_ref, g_ref, qkv_back, projected, gain_row, w_ref, grad_ref, stat_ref):
    up = g_ref[...].astype(F32)
    hg = mm(qkv_back, w_ref[...])
    normed, inverse = row_norm(u_ref[...].astype(F32))
    stat_ref[...] = jnp.concatenate([
        jnp.sum(hg, 0, keepdims=True),
        jnp.sum(hg * normed, 0, keepdims=True),
        jnp.sum(up * projected, 0, keepdims=True),
        gain_row, jnp.zeros((4, 1152), F32)], 0)
    ng = hg * scale1
    grad_ref[...] = (up + inverse * (
        ng - jnp.mean(ng, -1, keepdims=True)
        - normed * jnp.mean(ng * normed, -1, keepdims=True))).astype(BF)


def split_store(ref, value, width):
    ref[0] = value[:, 0:width]
    ref[1] = value[:, width:2 * width]


def temporal_kernel(ts_ref, time_ref, table_ref, gains_ref, w_hbm, wp_hbm, u_ref, g_ref, cos_ref, sin_ref,
                    out_ref, grad_ref, hid_ref, qkb_ref, pin_ref, atth_ref, stat_ref,
                    qkv_ref, dat_ref, mod_ref, w_ref, wp_ref, sem):
    loads = load_weights(1, w_hbm, wp_hbm, w_ref, wp_ref, sem)
    modulation(1, ts_ref, time_ref, table_ref, mod_ref)
    scale1 = 1.0 + mod_ref[1:2]
    loads[1].wait()
    before_heads(scale1, mod_ref, u_ref, g_ref, wp_ref, hid_ref, pin_ref, dat_ref)
    loads[0].wait()
    qkv_ref[...] = mm_nt(hid_ref[...], w_ref[...]).astype(BF)
    heads = Heads(True, gains_ref[1], (cos_ref[...], sin_ref[...]), qkv_ref, dat_ref)
    for h in range(8):
        heads.step(h)
    qkv_back = heads.qkv_back()
    attended = jnp.concatenate(heads.att, 1)
    split_store(qkb_ref, qkv_back, 864)
    split_store(atth_ref, attended, 288)
    projected = mm(attended, wp_ref[...])
    out_ref[...] = (u_ref[...].astype(F32) + mod_ref[2:3] * projected).astype(BF)
    after_heads(scale1, u_ref, g_ref, qkv_back, projected, heads.gain_row(), w_ref, grad_ref, stat_ref)


VM = pl.BlockSpec(memory_space=pltpu.VMEM)
HBM = pl.BlockSpec(memory_space=pl.ANY)
SMEM = pl.BlockSpec(memory_space=pltpu.SMEM)
PARAM_SPECS = [SMEM, VM, VM, VM, HBM, HBM]
LIMIT = 56 * 1024 * 1024
WEIGHT_SCRATCH = [pltpu.VMEM((3, 1152), F32), pltpu.VMEM((1728, 1152), BF),
                  pltpu.VMEM((576, 1152), BF), pltpu.SemaphoreType.DMA((2,))]


def sds(shape, dtype=BF):
    return jax.ShapeDtypeStruct(shape, dtype)


def call(kernel, outs, params, arrays, scratch, name):
    return pl.pallas_call(
        kernel, out_shape=outs, in_specs=PARAM_SPECS + [VM] * len(arrays), out_specs=(VM,) * len(outs),
        scratch_shapes=scratch + WEIGHT_SCRATCH,
        compiler_params=pltpu.CompilerParams(vmem_limit_bytes=LIMIT), name=name,
    )(*params, *arrays)


BACK_OUT = (sds((288, 1152)), sds((288, 1152)), sds((2, 288, 864)), sds((288, 1152)),
            sds((2, 288, 288)), sds((8, 1152), F32))


def rope_arrays():
    freq = np.power(10000.0, -2.0 * np.arange(36) / HD)
    angle = np.arange(96)[:, None] * freq[None]
    cosine = np.concatenate([np.cos(angle)] * 2, 1)
    sine = np.concatenate([-np.sin(angle), np.sin(angle)], 1)
    return (jnp.asarray(np.tile(cosine, (3, 1)), F32), jnp.asarray(np.tile(sine, (3, 1)), F32))


def spatial_forward(params, u):
    return call(forward_kernel, (sds((288, 1152)), sds((288, 1728)), sds((288, 576)), sds((3, 1152), F32)), params, (u,), [],
                "spatial_forward")


def temporal(params, u, g):
    half = pltpu.VMEM((288, 576), BF)
    return call(temporal_kernel, (sds((288, 1152)),) + BACK_OUT, params, (u, g) + rope_arrays(),
                [pltpu.VMEM((288, 1728), BF), half], "temporal")


def selector(rows, columns, place):
    at = lax.broadcasted_iota(jnp.int32, (rows, columns), 0)
    return jnp.where(lax.broadcasted_iota(jnp.int32, (rows, columns), 1) == place(at), 1.0, 0.0).astype(BF)


def pack(value, out_ref, count):
    def at(r, j):
        a = (r * 11) >> 5
        return 96 * a + 3 * j + r - 3 * a

    def first(i):
        r = i & 15
        return jnp.where(r < 9, at(r, i >> 4), -1)

    def second(i):
        r = i & 15
        return jnp.where(r >= 9, at(r - 9, i >> 4), -1)

    def third(i):
        r = i & 15
        return jnp.where(jnp.logical_or(r == 9, r == 10), at(r - 2, i >> 4), -1)
    s1 = selector(512, 288, first)
    tail = value[:, 768:1152]
    low = mm(s1, value[:, 0:384]) + mm(selector(512, 288, second), tail)
    high = mm(s1, value[:, 384:768]) + mm(selector(512, 288, third), tail)
    out_ref[:, :, 0:384] = low.astype(BF).reshape(32, 16, 384)
    out_ref[:, :, 384:768] = high.astype(BF).reshape(32, 16, 384)


def unpack(parcel_ref):
    def source(o):
        b = (o >= 96).astype(jnp.int32) + (o >= 192).astype(jnp.int32)
        rest = o - 96 * b
        i = (rest * 683) >> 11
        return 16 * i, 3 * (rest - 3 * i) + b

    def first(o):
        base, r = source(o)
        return base + r

    def second(o):
        base, r = source(o)
        return jnp.where(r < 7, base + 9 + r, -1)

    def third(o):
        base, r = source(o)
        return jnp.where(r >= 7, base + 2 + r, -1)
    low = parcel_ref[:, :, 0:384].reshape(512, 384)
    high = parcel_ref[:, :, 384:768].reshape(512, 384)
    t1 = selector(288, 512, first)
    tail = mm(selector(288, 512, second), low) + mm(selector(288, 512, third), high)
    return jnp.concatenate([mm(t1, low), mm(t1, high), tail], 1).astype(BF)


LA = 640
LB = 512


def place():
    dp = lax.axis_index("dp")
    seq = lax.axis_index("seq")
    return dp, seq, dp // 4, dp % 4, seq // 8, (seq // 2) % 4, seq % 2


def dev(dp, seq):
    return {"dp": dp, "seq": seq}


def remote(src, dst, send, recv, device):
    return pltpu.make_async_remote_copy(src_ref=src, dst_ref=dst, send_sem=send, recv_sem=recv,
                                        device_id=device, device_id_type=MESH)


class Sums:
    def __init__(self, sources, bufs, sems):
        self.hid, self.qkb, self.pin, self.att = sources
        (self.hid_s, self.qkb_s, self.pin_s, self.att_s, self.P, self.RA, self.RB, self.SA, self.SB,
         self.RA2, self.RB2, self.U, self.V, self.W, self.X) = bufs
        (self.act_send, self.act_recv, self.a_send, self.a_recv, self.b_send, self.b_recv, self.a2_send,
         self.a2_recv, self.b2_send, self.b2_recv, self.z_send, self.z_recv, self.f_send, self.f_recv) = sems
        self.dp, self.seq, self.z_hi, self.x, self.y, self.zl, self.c = place()
        self.z = self.z_hi * 4 + self.zl
        self.sib = self.y * 8 + self.zl * 2 + (1 - self.c)
        self.acts = []

    def at_x(self, k):
        return dev(self.z_hi * 4 + (self.x + k) % 4, self.seq)

    def at_y(self, k):
        return dev(self.dp, ((self.y + k) % 4) * 8 + self.zl * 2 + self.c)

    def start_act(self, i):
        src, dst = ((self.hid, self.hid_s), (self.qkb.at[1 - self.c], self.qkb_s),
                    (self.pin, self.pin_s), (self.att.at[1 - self.c], self.att_s))[i]
        self.acts.append(remote(src, dst, self.act_send.at[i], self.act_recv.at[i],
                                dev(self.dp, self.sib)))
        self.acts[-1].start()

    def products(self):
        for act in self.acts:
            act.wait()
        P, c = self.P, self.c

        def column_step(t, carry):
            lanes = pl.ds(pl.multiple_of(t * 384, 128), 384)
            acc = mm_tn(self.qkb[c], self.hid[:, lanes]) + mm_tn(self.qkb_s[...], self.hid_s[:, lanes])
            accp = mm_tn(self.att[c], self.pin[:, lanes]) + mm_tn(self.att_s[...], self.pin_s[:, lanes])
            for xo in range(4):
                for q in range(4):
                    if q < 3:
                        piece = acc[216 * xo + 72 * q: 216 * xo + 72 * q + 72]
                    else:
                        piece = accp[72 * xo: 72 * xo + 72]
                    P[xo, q, :, lanes] = jnp.concatenate(
                        [piece, jnp.zeros((8, 384), F32)], 0).astype(BF)
            return carry
        lax.fori_loop(0, 3, column_step, 0)
        self.ca, self.cb = [], []
        for k in range(1, 4):
            xx = (self.x + k) % 4
            yy = (self.y + k) % 4
            self.ca.append(remote(P.at[xx, :, :, pl.ds(0, LA)], self.RA.at[k - 1], self.a_send.at[k - 1],
                                  self.a_recv.at[k - 1], self.at_x(k)))
            self.cb.append(remote(P.at[:, yy, :, pl.ds(LA, LB)], self.RB.at[k - 1], self.b_send.at[k - 1],
                                  self.b_recv.at[k - 1], self.at_y(k)))
        for k in range(3):
            self.ca[k].start()
            self.cb[k].start()

    def first_sums(self):
        P, RA, RB, SA, SB, x, y = self.P, self.RA, self.RB, self.SA, self.SB, self.x, self.y
        for copy in self.cb:
            copy.wait()

        def sum_b(xo, carry):
            tot = P[xo, y, :, LA:LA + LB].astype(F32)
            for k in range(3):
                tot = tot + RB[k, xo].astype(F32)
            SB[xo] = tot.astype(BF)
            return carry
        lax.fori_loop(0, 4, sum_b, 0)
        self.second = []
        for k in range(1, 4):
            self.second.append(remote(SB.at[(x + k) % 4], self.RB2.at[k - 1], self.b2_send.at[k - 1],
                                      self.b2_recv.at[k - 1], self.at_x(k)))
            self.second[-1].start()
        for copy in self.ca:
            copy.wait()

        def sum_a(q, carry):
            tot = P[x, q, :, 0:LA].astype(F32)
            for k in range(3):
                tot = tot + RA[k, q].astype(F32)
            SA[q] = tot.astype(BF)
            return carry
        lax.fori_loop(0, 4, sum_a, 0)
        for k in range(1, 4):
            self.second.append(remote(SA.at[(y + k) % 4], self.RA2.at[k - 1], self.a2_send.at[k - 1],
                                      self.a2_recv.at[k - 1], self.at_y(k)))
            self.second[-1].start()

    def second_sums(self):
        for copy in self.second:
            copy.wait()
        ta = self.SA[self.y].astype(F32)
        tb = self.SB[self.x].astype(F32)
        for k in range(3):
            ta = ta + self.RA2[k].astype(F32)
            tb = tb + self.RB2[k].astype(F32)
        full = jnp.concatenate([ta, tb], 1)
        for j in range(4):
            self.U[j] = jnp.concatenate(
                [full[:, 72 * (4 * yy + j): 72 * (4 * yy + j) + 72] for yy in range(4)]
                + [jnp.zeros((80, 96), F32)], 1).astype(BF)
        for j in range(4):
            copy = remote(self.U.at[j], self.V.at[self.z], self.z_send.at[j], self.z_recv.at[self.z],
                          dev(self.c * 4 + self.x, self.y * 8 + j * 2 + self.c))

            @pl.when(self.c * 4 + j != self.z)
            def _(copy=copy):
                copy.start()

    def z_sums(self):
        U, V, W, X, y, z = self.U, self.V, self.W, self.X, self.y, self.z

        @pl.when(self.z_hi == self.c)
        def _():
            V[z] = U[self.zl]
            for s in range(8):
                @pl.when(s != z)
                def _(s=s):
                    remote(U.at[0], V.at[s], self.z_send.at[0], self.z_recv.at[s],
                           dev(self.dp, self.seq)).wait_recv()
            tot = V[0].astype(F32)
            for s in range(1, 8):
                tot = tot + V[s].astype(F32)
            for i in range(4):
                W[i] = jnp.concatenate([tot[:, 72 * i: 72 * i + 72], jnp.zeros((80, 56), F32)],
                                       1).astype(BF)
            for yy in range(4):
                for cc in range(2):
                    mine = jnp.logical_and(yy == y, cc == self.c)

                    @pl.when(jnp.logical_not(mine))
                    def _(yy=yy, cc=cc):
                        remote(W.at[yy], X.at[y], self.f_send.at[yy * 2 + cc], self.f_recv.at[y],
                               dev(self.dp, yy * 8 + self.zl * 2 + cc)).start()

                    @pl.when(mine)
                    def _(yy=yy):
                        X[y] = W[yy]

    def finish(self, b, factor, qkv_out, proj_out):
        U, V, W, X, y, c = self.U, self.V, self.W, self.X, self.y, self.c
        for q in range(4):
            @pl.when(jnp.logical_not(jnp.logical_and(q == y, c == self.z_hi)))
            def _(q=q):
                remote(W.at[0], X.at[q], self.f_send.at[0], self.f_recv.at[q],
                       dev(self.dp, self.seq)).wait_recv()
        stacked = jnp.concatenate([X[q, 0:72, :].astype(F32) for q in range(4)], 0)
        turned = jnp.transpose(stacked, (1, 0)) * factor
        own = jnp.where(c == 0, turned[0:36], turned[36:72])
        qkv_out[:, b] = own[:, 0:216]
        proj_out[:, b] = own[:, 216:288]
        for j in range(4):
            @pl.when(c * 4 + j != self.z)
            def _(j=j):
                remote(U.at[j], V.at[0], self.z_send.at[j], self.z_recv.at[0],
                       dev(self.dp, self.seq)).wait_send()

        @pl.when(self.z_hi == c)
        def _():
            for yy in range(4):
                for cc in range(2):
                    @pl.when(jnp.logical_not(jnp.logical_and(yy == y, cc == c)))
                    def _(yy=yy, cc=cc):
                        remote(W.at[yy], X.at[0], self.f_send.at[yy * 2 + cc], self.f_recv.at[0],
                               dev(self.dp, self.seq)).wait_send()


class Terms:
    def __init__(self, T, levels, send, recv):
        self.T, self.levels, self.send, self.recv = T, levels, send, recv
        dp, seq, z_hi, x, y, zl, c = place()
        z = z_hi * 4 + zl
        self.me = (c, x, y, z)
        self.targets = (
            [dev(dp, y * 8 + zl * 2 + (1 - c))],
            [dev(z_hi * 4 + (x + k) % 4, seq) for k in range(1, 4)],
            [dev(dp, ((y + k) % 4) * 8 + zl * 2 + c) for k in range(1, 4)],
            [dev((((z + k) % 8) // 4) * 4 + x, y * 8 + ((z + k) % 4) * 2 + c) for k in range(1, 8)])

    def start(self, level):
        slots, me = self.levels[level], self.me[level]
        slots[me] = self.T[...]
        self.copies = [remote(self.T, slots.at[me], self.send.at[level, k], self.recv.at[level, k], target)
                       for k, target in enumerate(self.targets[level])]
        for copy in self.copies:
            copy.start()

    def end(self, level):
        for copy in self.copies:
            copy.wait()
        slots = self.levels[level]
        total = slots[0]
        for k in range(1, slots.shape[0]):
            total = total + slots[k]
        self.T[...] = total


def greet(wide):
    dp, seq, z_hi, x, y, zl, c = place()
    barrier = pltpu.get_barrier_semaphore()
    peers = [dev(dp, (seq + k) % 32) for k in range(1, 32)]
    if wide:
        peers += [dev(z_hi * 4 + (x + k) % 4, seq) for k in range(1, 4)]
        peers += [dev((1 - z_hi) * 4 + x, y * 8 + k * 2 + c) for k in range(4)]
    for peer in peers:
        pl.semaphore_signal(barrier, inc=1, device_id=peer, device_id_type=MESH)
    return barrier, len(peers)


def exchange_start(parcel, landed, send, recv):
    dp = lax.axis_index("dp")
    seq = lax.axis_index("seq")
    copies = []
    for k in range(1, 32):
        to = (seq + k) % 32
        copies.append(remote(parcel.at[to], landed.at[seq], send.at[k], recv.at[k], dev(dp, to)))
        copies[-1].start()
    landed[seq] = parcel[seq]
    return copies


def exchange_kernel(u_ref, out_ref, parcel, landed, send, recv):
    barrier, count = greet(False)
    pack(u_ref[...], parcel, 32)
    pl.semaphore_wait(barrier, count)
    for copy in exchange_start(parcel, landed, send, recv):
        copy.wait()
    out_ref[...] = unpack(landed)


def exchange(u):
    return pl.pallas_call(
        exchange_kernel, out_shape=sds((288, 1152)), in_specs=[VM], out_specs=VM,
        scratch_shapes=[pltpu.VMEM((32, 16, 768), BF), pltpu.VMEM((32, 16, 768), BF),
                        pltpu.SemaphoreType.DMA((32,)), pltpu.SemaphoreType.DMA((32,))],
        compiler_params=pltpu.CompilerParams(collective_id=1, has_side_effects=True,
                                             vmem_limit_bytes=LIMIT),
        name="exchange",
    )(u)


def back_kernel(factor, w_hbm, wp_hbm, gains_ref, mod_ref, u_ref, qkv_ref, att_ref, mg_ref,
                hid1, qkb1, pin1, att1, stat1,
                grad_ref, qkv_out, proj_out, table_out, gain_out, *scratch):
    (parcel, landed, ex_send, ex_recv, g_ref, hid0, qkb0, pin0, att0, stat0, dat_ref,
     w_ref, wp_ref, w_sem, T, TC, TX, TY, TZ, t_send, t_recv) = scratch[:21]
    rest = scratch[21:]
    bufs = [[ref.at[b] for ref in rest[:15]] for b in range(2)]
    sems = [[ref.at[b] for ref in rest[15:]] for b in range(2)]
    barrier, count = greet(True)
    loads = load_weights(0, w_hbm, wp_hbm, w_ref, wp_ref, w_sem)
    early = Sums((hid0, qkb0, pin0, att0), bufs[0], sems[0])
    late = Sums((hid1, qkb1, pin1, att1), bufs[1], sems[1])
    terms = Terms(T, (TC, TX, TY, TZ), t_send, t_recv)
    pack(mg_ref[...], parcel, 32)
    split_store(att0, att_ref[...], 288)
    pl.semaphore_wait(barrier, count)
    moves = exchange_start(parcel, landed, ex_send, ex_recv)
    for i in range(4):
        late.start_act(i)
    early.start_act(3)
    late.products()
    scale1 = 1.0 + mod_ref[1:2]
    for copy in moves:
        copy.wait()
    g_ref[...] = unpack(landed)
    loads[1].wait()
    before_heads(scale1, mod_ref, u_ref, g_ref, wp_ref, hid0, pin0, dat_ref)
    early.start_act(0)
    early.start_act(2)
    heads = Heads(False, gains_ref[0], None, qkv_ref, dat_ref)
    for h in range(8):
        heads.step(h)
        if h == 3:
            late.first_sums()
    qkv_back = heads.qkv_back()
    split_store(qkb0, qkv_back, 864)
    early.start_act(1)
    late.second_sums()
    early.products()
    loads[0].wait()
    after_heads(scale1, u_ref, g_ref, qkv_back, mm(att_ref[...], wp_ref[...]), heads.gain_row(),
                w_ref, grad_ref, stat0)
    T[...] = jnp.concatenate([stat0[0:3], stat1[0:3], stat0[3:4], stat1[3:4]], 0)
    terms.start(0)
    late.z_sums()
    terms.end(0)
    terms.start(1)
    early.first_sums()
    terms.end(1)
    terms.start(2)
    late.finish(1, factor, qkv_out, proj_out)
    early.second_sums()
    terms.end(2)
    terms.start(3)
    early.z_sums()
    terms.end(3)
    total = T[...] * factor
    table_out[:, 0] = total[0:3]
    table_out[:, 1] = total[3:6]
    for b in range(2):
        gain_out[b] = jnp.concatenate([total[6 + b:7 + b, 0:72], total[6 + b:7 + b, 128:200]], 0)
    early.finish(0, factor, qkv_out, proj_out)


def back(params, factor, mod, u, qkv, att, middle_grad, late):
    dma = pltpu.SemaphoreType.DMA
    vm = pltpu.VMEM
    return pl.pallas_call(
        lambda *refs: back_kernel(factor, *refs),
        out_shape=(sds((288, 1152)), sds((36, 2, 216), F32), sds((36, 2, 72), F32),
                   sds((3, 2, 1152), F32), sds((2, 2, 72), F32)),
        in_specs=[HBM, HBM] + [VM] * 11, out_specs=(VM,) * 5,
        scratch_shapes=[
            vm((32, 16, 768), BF), vm((32, 16, 768), BF), dma((32,)), dma((32,)),
            vm((288, 1152), BF), vm((288, 1152), BF), vm((2, 288, 864), BF), vm((288, 1152), BF),
            vm((2, 288, 288), BF), vm((8, 1152), F32), vm((288, 576), BF),
            vm((1728, 1152), BF), vm((576, 1152), BF), dma((2,)),
            vm((8, 1152), F32), vm((2, 8, 1152), F32), vm((4, 8, 1152), F32), vm((4, 8, 1152), F32),
            vm((8, 8, 1152), F32), dma((4, 7)), dma((4, 7)),
            vm((2, 288, 1152), BF), vm((2, 288, 864), BF), vm((2, 288, 1152), BF), vm((2, 288, 288), BF),
            vm((2, 4, 4, 80, 1152), BF),
            vm((2, 3, 4, 80, LA), BF), vm((2, 3, 4, 80, LB), BF),
            vm((2, 4, 80, LA), BF), vm((2, 4, 80, LB), BF),
            vm((2, 3, 80, LA), BF), vm((2, 3, 80, LB), BF),
            vm((2, 4, 80, 384), BF), vm((2, 8, 80, 384), BF),
            vm((2, 4, 80, 128), BF), vm((2, 4, 80, 128), BF),
            dma((2, 4)), dma((2, 4)), dma((2, 3)), dma((2, 3)), dma((2, 3)), dma((2, 3)),
            dma((2, 3)), dma((2, 3)), dma((2, 3)), dma((2, 3)), dma((2, 4)), dma((2, 8)),
            dma((2, 8)), dma((2, 4)),
        ],
        compiler_params=pltpu.CompilerParams(
            collective_id=0, has_side_effects=True, vmem_limit_bytes=LIMIT),
        name="back",
    )(params[4], params[5], params[3], mod, u, qkv, att, middle_grad, *late)


def local(tokens, timestep, time_table, block_tables, qk_gains, qkv_weight, proj_weight, cotangent):
    frame_dev, spatial, features = tokens.shape[1:]
    shape = (1, frame_dev, spatial, features)
    count = lax.axis_size("dp") * lax.axis_size("seq") * frame_dev * spatial
    params = (timestep, jnp.swapaxes(time_table, 0, 1), jnp.swapaxes(block_tables, 0, 1), qk_gains,
              jnp.swapaxes(qkv_weight, 1, 2), jnp.swapaxes(proj_weight, 1, 2))
    u = tokens.reshape(288, 1152)
    middle, qkv, att, mod = spatial_forward(params, u)
    block_out, middle_grad, *late = temporal(params, exchange(middle), cotangent.reshape(288, 1152))
    token_grad, qkv_grad, proj_grad, table_grad, gain_grad = back(
        params, 1.0 / math.sqrt(count), mod, u, qkv, att, middle_grad, late)
    return (block_out.reshape(shape), token_grad.reshape(shape), jnp.swapaxes(qkv_grad, 0, 1),
            jnp.swapaxes(proj_grad, 0, 1), jnp.swapaxes(table_grad, 0, 1), gain_grad)


def solution(mesh):
    return jax.shard_map(
        local,
        mesh=mesh,
        in_specs=(
            PS("dp", "seq", None, None),
            PS("dp"),
            PS(),
            PS(),
            PS(),
            PS(),
            PS(),
            PS("dp", "seq", None, None),
        ),
        out_specs=(
            PS("dp", "seq", None, None),
            PS("dp", "seq", None, None),
            PS(None, "seq", "dp"),
            PS(None, "seq", "dp"),
            PS(),
            PS(),
        ),
        check_vma=False,
    )
```

```python
import math

import numpy as np
import jax
import jax.numpy as jnp
from jax import lax
from jax.experimental import pallas as pl
from jax.experimental.pallas import tpu as pltpu
from jax.sharding import PartitionSpec as PS

MESH = pl.DeviceIdType.MESH

HD = 72
EPS = 1e-06
F32 = jnp.float32
BF = jnp.bfloat16
SCALE = 1.0 / math.sqrt(HD)


def mm(a, b):
    return lax.dot_general(a, b, (((1,), (0,)), ((), ())), preferred_element_type=F32)


def mm_nt(a, b):
    return lax.dot_general(a, b, (((1,), (1,)), ((), ())), preferred_element_type=F32)


def mm_tn(a, b):
    return lax.dot_general(a, b, (((0,), (0,)), ((), ())), preferred_element_type=F32)


def row_norm(u):
    center = u - jnp.mean(u, -1, keepdims=True)
    inverse = lax.rsqrt(jnp.mean(center * center, -1, keepdims=True) + EPS)
    return center * inverse, inverse


def wide_gain(gain):
    none = jnp.zeros((1, 56), F32)
    return (jnp.concatenate([gain, none], 1),
            jnp.concatenate([gain[:, 36:72], gain[:, 0:36], none], 1))


def fill_grid(grid_ref):
    row = lax.broadcasted_iota(jnp.int32, (384, 256), 0) - 128
    column = lax.broadcasted_iota(jnp.int32, (384, 256), 1)
    second = column - 128
    partner = jnp.where(second < 36, second + 36, second - 36)
    wanted = jnp.where(column < 72, column,
                       jnp.where(jnp.logical_and(second >= 0, second < 72), partner, -1000))
    grid_ref[...] = jnp.where(row == wanted, 1.0, 0.0).astype(F32)


def placed(ref, index, grid_ref, width):
    start = 72 * index
    a = start // 128 * 128
    off = start - a
    size = 128 if off + 72 <= 128 else min(256, ref.shape[1] - a)
    return mm(ref[:, a:a + size], grid_ref[128 - off:128 - off + size, 0:width].astype(BF))


def unit_of(wide):
    factor = lax.rsqrt(jnp.sum(wide * wide, -1, keepdims=True) * (1.0 / HD) + EPS)
    return wide * factor, factor


def unit_back(grad, unit, factor):
    return factor * (grad - unit * (jnp.sum(grad * unit, -1, keepdims=True) * (1.0 / HD)))


def softmax(qh, kh):
    e = jnp.exp(mm_nt(qh, kh) * SCALE)
    return e / jnp.sum(e, -1, keepdims=True)


def modulation(ts_ref, time_ref, table_ref, mod_ref):
    chosen = lax.broadcasted_iota(jnp.int32, (16, 1152), 0) == ts_ref[0]
    for i in range(3):
        row = jnp.sum(jnp.where(chosen, time_ref[i], 0.0), 0, keepdims=True)
        for block in range(2):
            mod_ref[block, i:i + 1] = table_ref[i, block:block + 1] + row


def hidden_of(normed, mod_ref):
    return (normed * (1.0 + mod_ref[1:2]) + mod_ref[0:1]).astype(BF)


def spatial_forward(u, mod_ref, gain_ref, w_ref, wp_ref, loads, hid_ref, qkv_ref, heads_ref, att_ref, grid_ref):
    normed, _ = row_norm(u)
    hid_ref[...] = hidden_of(normed, mod_ref)
    loads[0].wait()
    qkv_ref[...] = mm_nt(hid_ref[...], w_ref[...]).astype(BF)
    for i in range(24):
        heads_ref[i] = placed(qkv_ref, i, grid_ref, 128).astype(BF)
    gain_q, _ = wide_gain(gain_ref[0:1])
    gain_k, _ = wide_gain(gain_ref[1:2])
    parts = []
    for h in range(8):
        qh = (unit_of(heads_ref[h].astype(F32))[0] * gain_q).astype(BF)
        kh = (unit_of(heads_ref[8 + h].astype(F32))[0] * gain_k).astype(BF)
        v = heads_ref[16 + h]
        rows = []
        for g in range(3):
            s = slice(96 * g, 96 * g + 96)
            rows.append(mm(softmax(qh[s], kh[s]).astype(BF), v[s]))
        parts.append(jnp.concatenate(rows, 0).astype(BF)[:, 0:72])
    att_ref[...] = jnp.concatenate(parts, 1)
    loads[1].wait()
    return (u + mod_ref[2:3] * mm(att_ref[...], wp_ref[...])).astype(BF)


class Heads:
    def __init__(self, forward, gain, rope, fetch, dat_ref, grid_ref):
        self.forward, self.rope, self.fetch, self.dat_ref, self.grid_ref = forward, rope, fetch, dat_ref, grid_ref
        self.att, self.back = [], ([], [], [])
        self.gain, partner = zip(wide_gain(gain[0:1]), wide_gain(gain[1:2]))
        if rope is not None:
            cosine, sine = rope
            self.turn = [(cosine * self.gain[i], sine * partner[i]) for i in range(2)]
            self.turn_back = (cosine * SCALE, sine * SCALE)
            self.swap = grid_ref[128:256, 128:256].astype(BF)
        self.gq = jnp.zeros((1, 128), F32)
        self.gk = jnp.zeros((1, 128), F32)

    def norm(self, index, which):
        raw = self.fetch(index)
        unit, factor = unit_of(raw[:, 0:128])
        if self.rope is None:
            half = (unit * self.gain[which]).astype(BF)
            return unit, factor, half, half
        straight, crossed = self.turn[which]
        half = (factor * (raw[:, 0:128] * straight + raw[:, 128:256] * crossed)).astype(BF)
        return unit, factor, half, jnp.concatenate([half, mm(half, self.swap).astype(BF)], 1)

    def back_turn(self, grads):
        grad = jnp.concatenate(grads, 0)
        if self.rope is None:
            return grad * SCALE
        return grad[:, 0:128] * self.turn_back[0] - grad[:, 128:256] * self.turn_back[1]

    def step(self, h):
        qu, qf, qh, qx = self.norm(h, 0)
        ku, kf, kh, kx = self.norm(8 + h, 1)
        v = self.fetch(16 + h)[:, 0:128].astype(BF)
        da = placed(self.dat_ref, h, self.grid_ref, 128).astype(BF)
        avs, dqs, dks, dvs = [], [], [], []
        for g in range(3):
            s = slice(96 * g, 96 * g + 96)
            att = softmax(qh[s], kh[s])
            att16 = att.astype(BF)
            if self.forward:
                avs.append(mm(att16, v[s]))
            dp = mm_nt(da[s], v[s])
            dvs.append(mm_tn(att16, da[s]))
            ds = (att * (dp - jnp.sum(dp * att, -1, keepdims=True))).astype(BF)
            dqs.append(mm(ds, kx[s]))
            dks.append(mm_tn(ds, qx[s]))
        if self.forward:
            self.att.append(jnp.concatenate(avs, 0).astype(BF)[:, 0:72])
        dq = self.back_turn(dqs)
        dk = self.back_turn(dks)
        self.gq = self.gq + jnp.sum(dq * qu, 0, keepdims=True)
        self.gk = self.gk + jnp.sum(dk * ku, 0, keepdims=True)
        self.back[0].append(unit_back(dq * self.gain[0], qu, qf).astype(BF)[:, 0:72])
        self.back[1].append(unit_back(dk * self.gain[1], ku, kf).astype(BF)[:, 0:72])
        self.back[2].append(jnp.concatenate(dvs, 0).astype(BF)[:, 0:72])

    def qkv_back(self):
        return jnp.concatenate(self.back[0] + self.back[1] + self.back[2], 1)

    def gain_row(self):
        return jnp.concatenate([self.gq, self.gk, jnp.zeros((1, 1152 - 256), F32)], 1)


def after_heads(scale1, u_ref, g_ref, qkv_back, projected, gain_row, w_ref, grad_ref, stat_ref):
    up = g_ref[...].astype(F32)
    hg = mm(qkv_back, w_ref[...])
    normed, inverse = row_norm(u_ref[...].astype(F32))
    stat_ref[...] = jnp.concatenate([
        jnp.sum(hg, 0, keepdims=True),
        jnp.sum(hg * normed, 0, keepdims=True),
        jnp.sum(up * projected, 0, keepdims=True),
        gain_row, jnp.zeros((4, 1152), F32)], 0)
    ng = hg * scale1
    grad_ref[...] = (up + inverse * (
        ng - jnp.mean(ng, -1, keepdims=True)
        - normed * jnp.mean(ng * normed, -1, keepdims=True))).astype(BF)


def split_store(ref, value, width):
    ref[0] = value[:, 0:width]
    ref[1] = value[:, width:2 * width]


VM = pl.BlockSpec(memory_space=pltpu.VMEM)
HBM = pl.BlockSpec(memory_space=pl.ANY)
SMEM = pl.BlockSpec(memory_space=pltpu.SMEM)
LIMIT = 60 * 1024 * 1024


def sds(shape, dtype=BF):
    return jax.ShapeDtypeStruct(shape, dtype)


def rope_arrays():
    freq = np.power(10000.0, -2.0 * np.arange(36) / HD)
    angle = np.arange(96)[:, None] * freq[None]
    none = np.zeros((96, 56))
    cosine = np.concatenate([np.cos(angle), np.cos(angle), none], 1)
    sine = np.concatenate([-np.sin(angle), np.sin(angle), none], 1)
    return (jnp.asarray(np.tile(cosine, (3, 1)), F32), jnp.asarray(np.tile(sine, (3, 1)), F32))


def selector(rows, columns, place):
    at = lax.broadcasted_iota(jnp.int32, (rows, columns), 0)
    return jnp.where(lax.broadcasted_iota(jnp.int32, (rows, columns), 1) == place(at), 1.0, 0.0).astype(BF)


def fill_selectors(into_ref, from_ref):
    def at(r, j):
        a = (r * 11) >> 5
        return 96 * a + 3 * j + r - 3 * a

    def into(test, shift):
        def find(i):
            r = i & 15
            return jnp.where(test(r), at(r - shift, i >> 4), -1)
        return find

    for k, (test, shift) in enumerate((
            (lambda r: r < 9, 0), (lambda r: r >= 9, 9),
            (lambda r: jnp.logical_or(r == 9, r == 10), 2),
            (lambda r: jnp.logical_or(r == 11, r == 12), 4))):
        into_ref[k] = selector(512, 288, into(test, shift))

    def back(low, shift):
        def find(o):
            b = (o >= 96).astype(jnp.int32) + (o >= 192).astype(jnp.int32)
            rest = o - 96 * b
            i = (rest * 683) >> 11
            r = 3 * (rest - 3 * i) + b
            place = 16 * i + r + shift
            if low is None:
                return place
            return jnp.where((r < 7) == low, place, -1)
        return find
    for k, (low, shift) in enumerate(((None, 0), (True, 9), (False, 2), (False, 4))):
        from_ref[k] = selector(288, 512, back(low, shift))


def pack(value, out_ref, into):
    tail = value[:, 768:1152]
    low = mm(into[0], value[:, 0:384]) + mm(into[1], tail)
    high = mm(into[0], value[:, 384:768]) + mm(into[2], tail)
    out_ref[:, :, 0:384] = low.astype(BF).reshape(32, 16, 384)
    out_ref[:, :, 384:768] = high.astype(BF).reshape(32, 16, 384)


def unpack(parcel_ref, back):
    low = parcel_ref[:, :, 0:384].reshape(512, 384)
    high = parcel_ref[:, :, 384:768].reshape(512, 384)
    tail = mm(back[1], low) + mm(back[2], high)
    return jnp.concatenate([mm(back[0], low), mm(back[0], high), tail], 1).astype(BF)


def pack_half(value, out_ref, into):
    tail = jnp.concatenate([value[:, 384:576], jnp.zeros((288, 64), BF)], 1)
    low = mm(into[0], value[:, 0:256]) + mm(into[1], tail)
    high = mm(into[0], value[:, 256:384]) + mm(into[2], tail[:, 0:128]) + mm(into[3], tail[:, 128:256])
    out_ref[:, :, 0:256] = low.astype(BF).reshape(32, 16, 256)
    out_ref[:, :, 256:384] = high.astype(BF).reshape(32, 16, 128)


def unpack_half(parcel_ref, back):
    low = parcel_ref[:, :, 0:256].reshape(512, 256)
    high = parcel_ref[:, :, 256:384].reshape(512, 128)
    tail = mm(back[1], low) + jnp.concatenate([mm(back[2], high), mm(back[3], high)], 1)
    return jnp.concatenate([mm(back[0], low), mm(back[0], high), tail[:, 0:192]], 1).astype(BF)


LA = 640
LB = 512


def place():
    dp = lax.axis_index("dp")
    seq = lax.axis_index("seq")
    return dp, seq, dp // 4, dp % 4, seq // 8, (seq // 2) % 4, seq % 2


def dev(dp, seq):
    return {"dp": dp, "seq": seq}


def remote(src, dst, send, recv, device):
    return pltpu.make_async_remote_copy(src_ref=src, dst_ref=dst, send_sem=send, recv_sem=recv,
                                        device_id=device, device_id_type=MESH)


class Sums:
    def __init__(self, sources, bufs, sems):
        self.hid, self.qkb, self.pin, self.att = sources
        (self.hid_s, self.qkb_s, self.pin_s, self.att_s, self.P, self.RA, self.RB, self.SA, self.SB,
         self.RA2, self.RB2, self.U, self.V, self.W, self.X) = bufs
        (self.act_send, self.act_recv, self.a_send, self.a_recv, self.b_send, self.b_recv, self.a2_send,
         self.a2_recv, self.b2_send, self.b2_recv, self.z_send, self.z_recv, self.f_send, self.f_recv) = sems
        self.dp, self.seq, self.z_hi, self.x, self.y, self.zl, self.c = place()
        self.z = self.z_hi * 4 + self.zl
        self.sib = self.y * 8 + self.zl * 2 + (1 - self.c)
        self.acts = {}

    def at_x(self, k):
        return dev(self.z_hi * 4 + (self.x + k) % 4, self.seq)

    def at_y(self, k):
        return dev(self.dp, ((self.y + k) % 4) * 8 + self.zl * 2 + self.c)

    def start_act(self, i):
        src, dst = ((self.hid, self.hid_s), (self.qkb.at[1 - self.c], self.qkb_s),
                    (self.pin, self.pin_s), (self.att.at[1 - self.c], self.att_s))[i]
        self.acts[i] = remote(src, dst, self.act_send.at[i], self.act_recv.at[i], dev(self.dp, self.sib))
        self.acts[i].start()

    def products_qkv(self):
        for act in (0, 1):
            self.acts[act].wait()
        P, c = self.P, self.c

        def column_step(t, carry):
            lanes = pl.ds(pl.multiple_of(t * 384, 128), 384)
            acc = mm_tn(self.qkb[c], self.hid[:, lanes]) + mm_tn(self.qkb_s[...], self.hid_s[:, lanes])
            for xo in range(4):
                for q in range(3):
                    piece = acc[216 * xo + 72 * q: 216 * xo + 72 * q + 72]
                    P[xo, q, :, lanes] = jnp.concatenate([piece, jnp.zeros((8, 384), F32)], 0).astype(BF)
            return carry
        lax.fori_loop(0, 3, column_step, 0)
        self.ca, self.cb = [], []
        for k in range(1, 4):
            xx = (self.x + k) % 4
            yy = (self.y + k) % 4
            self.ca.append(remote(P.at[xx, pl.ds(0, 3), :, pl.ds(0, LA)], self.RA.at[k - 1, pl.ds(0, 3)],
                                  self.a_send.at[k - 1], self.a_recv.at[k - 1], self.at_x(k)))
            self.cb.append(remote(P.at[:, yy, :, pl.ds(LA, LB)], self.RB.at[k - 1], self.b_send.at[k - 1],
                                  self.b_recv.at[k - 1], self.at_y(k)))
        for k in range(3):
            self.ca[k].start()

            @pl.when((self.y + k + 1) % 4 != 3)
            def _(k=k):
                self.cb[k].start()

    def products_proj(self):
        for act in (2, 3):
            self.acts[act].wait()
        P, c = self.P, self.c

        def column_step(t, carry):
            lanes = pl.ds(pl.multiple_of(t * 384, 128), 384)
            acc = mm_tn(self.att[c], self.pin[:, lanes]) + mm_tn(self.att_s[...], self.pin_s[:, lanes])
            for xo in range(4):
                P[xo, 3, :, lanes] = jnp.concatenate(
                    [acc[72 * xo: 72 * xo + 72], jnp.zeros((8, 384), F32)], 0).astype(BF)
            return carry
        lax.fori_loop(0, 3, column_step, 0)
        for k in range(1, 4):
            xx = (self.x + k) % 4
            self.ca.append(remote(P.at[xx, 3, :, pl.ds(0, LA)], self.RA.at[k - 1, 3],
                                  self.a_send.at[k + 2], self.a_recv.at[k + 2], self.at_x(k)))
            self.ca[-1].start()

            @pl.when((self.y + k) % 4 == 3)
            def _(k=k):
                self.cb[k - 1].start()

    def first_sums(self):
        P, RA, RB, SA, SB, x, y = self.P, self.RA, self.RB, self.SA, self.SB, self.x, self.y
        for copy in self.cb:
            copy.wait()

        def sum_b(xo, carry):
            tot = P[xo, y, :, LA:LA + LB].astype(F32)
            for k in range(3):
                tot = tot + RB[k, xo].astype(F32)
            SB[xo] = tot.astype(BF)
            return carry
        lax.fori_loop(0, 4, sum_b, 0)
        self.second = []
        for k in range(1, 4):
            self.second.append(remote(SB.at[(x + k) % 4], self.RB2.at[k - 1], self.b2_send.at[k - 1],
                                      self.b2_recv.at[k - 1], self.at_x(k)))
            self.second[-1].start()
        for copy in self.ca:
            copy.wait()

        def sum_a(q, carry):
            tot = P[x, q, :, 0:LA].astype(F32)
            for k in range(3):
                tot = tot + RA[k, q].astype(F32)
            SA[q] = tot.astype(BF)
            return carry
        lax.fori_loop(0, 4, sum_a, 0)
        for k in range(1, 4):
            self.second.append(remote(SA.at[(y + k) % 4], self.RA2.at[k - 1], self.a2_send.at[k - 1],
                                      self.a2_recv.at[k - 1], self.at_y(k)))
            self.second[-1].start()

    def second_sums(self):
        for copy in self.second:
            copy.wait()
        ta = self.SA[self.y].astype(F32)
        tb = self.SB[self.x].astype(F32)
        for k in range(3):
            ta = ta + self.RA2[k].astype(F32)
            tb = tb + self.RB2[k].astype(F32)
        full = jnp.concatenate([ta, tb], 1)
        for j in range(4):
            self.U[j] = jnp.concatenate(
                [full[:, 72 * (4 * yy + j): 72 * (4 * yy + j) + 72] for yy in range(4)]
                + [jnp.zeros((80, 96), F32)], 1).astype(BF)
        for j in range(4):
            copy = remote(self.U.at[j], self.V.at[self.z], self.z_send.at[j], self.z_recv.at[self.z],
                          dev(self.c * 4 + self.x, self.y * 8 + j * 2 + self.c))

            @pl.when(self.c * 4 + j != self.z)
            def _(copy=copy):
                copy.start()

    def z_sums(self):
        U, V, W, X, y, z = self.U, self.V, self.W, self.X, self.y, self.z

        @pl.when(self.z_hi == self.c)
        def _():
            V[z] = U[self.zl]
            for s in range(8):
                @pl.when(s != z)
                def _(s=s):
                    remote(U.at[0], V.at[s], self.z_send.at[0], self.z_recv.at[s],
                           dev(self.dp, self.seq)).wait_recv()
            tot = V[0].astype(F32)
            for s in range(1, 8):
                tot = tot + V[s].astype(F32)
            for i in range(4):
                W[i] = jnp.concatenate([tot[:, 72 * i: 72 * i + 72], jnp.zeros((80, 56), F32)],
                                       1).astype(BF)
            for yy in range(4):
                for cc in range(2):
                    mine = jnp.logical_and(yy == y, cc == self.c)

                    @pl.when(jnp.logical_not(mine))
                    def _(yy=yy, cc=cc):
                        remote(W.at[yy], X.at[y], self.f_send.at[yy * 2 + cc], self.f_recv.at[y],
                               dev(self.dp, yy * 8 + self.zl * 2 + cc)).start()

                    @pl.when(mine)
                    def _(yy=yy):
                        X[y] = W[yy]

    def finish(self, b, factor, qkv_out, proj_out):
        U, V, W, X, y, c = self.U, self.V, self.W, self.X, self.y, self.c
        for q in range(4):
            @pl.when(jnp.logical_not(jnp.logical_and(q == y, c == self.z_hi)))
            def _(q=q):
                remote(W.at[0], X.at[q], self.f_send.at[0], self.f_recv.at[q],
                       dev(self.dp, self.seq)).wait_recv()
        stacked = jnp.concatenate([X[q, 0:72, :].astype(F32) for q in range(4)], 0)
        turned = jnp.transpose(stacked, (1, 0)) * factor
        own = jnp.where(c == 0, turned[0:36], turned[36:72])
        qkv_out[:, b] = own[:, 0:216]
        proj_out[:, b] = own[:, 216:288]
        for j in range(4):
            @pl.when(c * 4 + j != self.z)
            def _(j=j):
                remote(U.at[j], V.at[0], self.z_send.at[j], self.z_recv.at[0],
                       dev(self.dp, self.seq)).wait_send()

        @pl.when(self.z_hi == c)
        def _():
            for yy in range(4):
                for cc in range(2):
                    @pl.when(jnp.logical_not(jnp.logical_and(yy == y, cc == c)))
                    def _(yy=yy, cc=cc):
                        remote(W.at[yy], X.at[0], self.f_send.at[yy * 2 + cc], self.f_recv.at[0],
                               dev(self.dp, self.seq)).wait_send()


class Terms:
    def __init__(self, T, levels, send, recv):
        self.T, self.levels, self.send, self.recv = T, levels, send, recv
        dp, seq, z_hi, x, y, zl, c = place()
        z = z_hi * 4 + zl
        self.me = (c, x, y, z)
        self.targets = (
            [dev(dp, y * 8 + zl * 2 + (1 - c))],
            [dev(z_hi * 4 + (x + k) % 4, seq) for k in range(1, 4)],
            [dev(dp, ((y + k) % 4) * 8 + zl * 2 + c) for k in range(1, 4)],
            [dev((((z + k) % 8) // 4) * 4 + x, y * 8 + ((z + k) % 4) * 2 + c) for k in range(1, 8)])

    def start(self, level):
        slots, me = self.levels[level], self.me[level]
        slots[me] = self.T[...]
        self.copies = [remote(self.T, slots.at[me], self.send.at[level, k], self.recv.at[level, k], target)
                       for k, target in enumerate(self.targets[level])]
        for copy in self.copies:
            copy.start()

    def end(self, level):
        for copy in self.copies:
            copy.wait()
        slots = self.levels[level]
        total = slots[0]
        for k in range(1, slots.shape[0]):
            total = total + slots[k]
        self.T[...] = total


def greet():
    dp, seq, z_hi, x, y, zl, c = place()
    barrier = pltpu.get_barrier_semaphore()
    peers = [dev(dp, (seq + k) % 32) for k in range(1, 32)]
    peers += [dev(z_hi * 4 + (x + k) % 4, seq) for k in range(1, 4)]
    peers += [dev((1 - z_hi) * 4 + x, y * 8 + k * 2 + c) for k in range(4)]
    for peer in peers:
        pl.semaphore_signal(barrier, inc=1, device_id=peer, device_id_type=MESH)
    return barrier, len(peers)


def exchange_start(parcel, landed, send, recv):
    dp = lax.axis_index("dp")
    seq = lax.axis_index("seq")
    copies = []
    for k in range(1, 32):
        to = (seq + k) % 32
        copies.append(remote(parcel.at[to], landed.at[seq], send.at[k], recv.at[k], dev(dp, to)))
        copies[-1].start()
    landed[seq] = parcel[seq]
    return copies


def pair_kernel(factor, ts_ref, w_hbm, wp_hbm, time_ref, table_ref, gains_ref, u_ref, cot_ref, cos_ref, sin_ref,
                out_ref, grad_ref, qkv_out, proj_out, table_out, gain_out, *scratch):
    (parcel, landed, halfp, half_landed, ex_send, ex_recv, into, back, mod_ref, qkv_ref, heads_ref, att_ref,
     u1_ref, mg_ref, dat_ref, hid, qkb, pin, att, stat, grid_ref, w_ref, wp_ref, w_sem,
     T, TC, TX, TY, TZ, t_send, t_recv) = scratch[:31]
    rest = scratch[31:]
    loads = []
    for block in range(2):
        loads.append([pltpu.make_async_copy(w_hbm.at[block], w_ref.at[block], w_sem.at[block, 0]),
                      pltpu.make_async_copy(wp_hbm.at[block], wp_ref.at[block], w_sem.at[block, 1])])
        for load in loads[-1]:
            load.start()
    barrier, count = greet()
    sums = [Sums([ref.at[b] for ref in (hid, qkb, pin, att)], [ref.at[b] for ref in rest[:15]],
                 [ref.at[b] for ref in rest[15:]]) for b in range(2)]
    early, late = sums
    terms = Terms(T, (TC, TX, TY, TZ), t_send, t_recv)
    fill_grid(grid_ref)
    fill_selectors(into, back)
    modulation(ts_ref, time_ref, table_ref, mod_ref)
    mods = [mod_ref.at[b] for b in range(2)]

    pack(spatial_forward(u_ref[...].astype(F32), mods[0], gains_ref.at[0], w_ref.at[0], wp_ref.at[0], loads[0],
                         hid.at[0], qkv_ref, heads_ref, att_ref, grid_ref), parcel, into)
    pl.semaphore_wait(barrier, count)
    moves = exchange_start(parcel, landed.at[0], ex_send.at[0], ex_recv.at[0])
    split_store(att.at[0], att_ref[...], 288)
    early.start_act(0)
    early.start_act(3)
    gate = mods[1][2:3]
    pin[1] = (cot_ref[...].astype(F32) * gate).astype(BF)
    late.start_act(2)
    loads[1][1].wait()
    dat_ref[...] = mm_nt(pin[1], wp_ref[1]).astype(BF)
    for copy in moves:
        copy.wait()
    u1_ref[...] = unpack(landed.at[0], back)

    normed, _ = row_norm(u1_ref[...].astype(F32))
    hid[1] = hidden_of(normed, mods[1])
    late.start_act(0)
    loads[1][0].wait()
    qkv_ref[...] = mm_nt(hid[1], w_ref[1]).astype(BF)
    heads = Heads(True, gains_ref[1], (cos_ref[...], sin_ref[...]),
                  lambda i: placed(qkv_ref, i, grid_ref, 256 if i < 16 else 128), dat_ref, grid_ref)
    for h in range(8):
        heads.step(h)
    qkv_back = heads.qkv_back()
    attended = jnp.concatenate(heads.att, 1)
    split_store(qkb.at[1], qkv_back, 864)
    split_store(att.at[1], attended, 288)
    late.start_act(1)
    late.start_act(3)
    projected = mm(attended, wp_ref[1])
    out_ref[...] = (u1_ref[...].astype(F32) + gate * projected).astype(BF)
    after_heads(1.0 + mods[1][1:2], u1_ref, cot_ref, qkv_back, projected, heads.gain_row(), w_ref.at[1],
                mg_ref, stat.at[1])

    gate = mods[0][2:3]
    head_grad = mm_nt((mg_ref[...].astype(F32) * gate).astype(BF), wp_ref[0]).astype(BF)
    pack_half(head_grad, halfp, into)
    half_moves = exchange_start(halfp, half_landed, ex_send.at[1], ex_recv.at[1])
    pack(mg_ref[...], parcel, into)
    moves = exchange_start(parcel, landed.at[1], ex_send.at[2], ex_recv.at[2])
    late.products_qkv()
    late.products_proj()
    for copy in half_moves:
        copy.wait()
    dat_ref[...] = unpack_half(half_landed, back)
    heads = Heads(False, gains_ref[0], None, lambda i: heads_ref[i].astype(F32), dat_ref, grid_ref)
    for h in range(8):
        heads.step(h)
    qkv_back = heads.qkv_back()
    split_store(qkb.at[0], qkv_back, 864)
    early.start_act(1)
    for copy in moves:
        copy.wait()
    u1_ref[...] = unpack(landed.at[1], back)
    pin[0] = (u1_ref[...].astype(F32) * gate).astype(BF)
    early.start_act(2)
    early.products_qkv()
    late.first_sums()
    early.products_proj()
    after_heads(1.0 + mods[0][1:2], u_ref, u1_ref, qkv_back, mm(att_ref[...], wp_ref[0]), heads.gain_row(),
                w_ref.at[0], grad_ref, stat.at[0])
    late.second_sums()
    T[...] = jnp.concatenate([stat[0, 0:3], stat[1, 0:3], stat[0, 3:4], stat[1, 3:4]], 0)
    terms.start(0)
    late.z_sums()
    terms.end(0)
    terms.start(1)
    early.first_sums()
    terms.end(1)
    terms.start(2)
    late.finish(1, factor, qkv_out, proj_out)
    early.second_sums()
    terms.end(2)
    terms.start(3)
    early.z_sums()
    terms.end(3)
    total = T[...] * factor
    table_out[:, 0] = total[0:3]
    table_out[:, 1] = total[3:6]
    for b in range(2):
        gain_out[b] = jnp.concatenate([total[6 + b:7 + b, 0:72], total[6 + b:7 + b, 128:200]], 0)
    early.finish(0, factor, qkv_out, proj_out)


def block_pair(factor, timestep, qkv_weight, proj_weight, time_table, block_tables, qk_gains, u, cotangent):
    dma = pltpu.SemaphoreType.DMA
    vm = pltpu.VMEM
    return pl.pallas_call(
        lambda *refs: pair_kernel(factor, *refs),
        out_shape=(sds((288, 1152)), sds((288, 1152)), sds((36, 2, 216), F32), sds((36, 2, 72), F32),
                   sds((3, 2, 1152), F32), sds((2, 2, 72), F32)),
        in_specs=[SMEM, HBM, HBM] + [VM] * 7, out_specs=(VM,) * 6,
        scratch_shapes=[
            vm((32, 16, 768), BF), vm((2, 32, 16, 768), BF), vm((32, 16, 384), BF), vm((32, 16, 384), BF),
            dma((3, 32)), dma((3, 32)), vm((4, 512, 288), BF), vm((4, 288, 512), BF), vm((2, 3, 1152), F32),
            vm((288, 1728), BF), vm((24, 288, 128), BF), vm((288, 576), BF),
            vm((288, 1152), BF), vm((288, 1152), BF), vm((288, 576), BF),
            vm((2, 288, 1152), BF), vm((2, 2, 288, 864), BF), vm((2, 288, 1152), BF), vm((2, 2, 288, 288), BF),
            vm((2, 8, 1152), F32), vm((384, 256), F32),
            vm((2, 1728, 1152), BF), vm((2, 576, 1152), BF), dma((2, 2)),
            vm((8, 1152), F32), vm((2, 8, 1152), F32), vm((4, 8, 1152), F32), vm((4, 8, 1152), F32),
            vm((8, 8, 1152), F32), dma((4, 7)), dma((4, 7)),
            vm((2, 288, 1152), BF), vm((2, 288, 864), BF), vm((2, 288, 1152), BF), vm((2, 288, 288), BF),
            vm((2, 4, 4, 80, 1152), BF),
            vm((2, 3, 4, 80, LA), BF), vm((2, 3, 4, 80, LB), BF),
            vm((2, 4, 80, LA), BF), vm((2, 4, 80, LB), BF),
            vm((2, 3, 80, LA), BF), vm((2, 3, 80, LB), BF),
            vm((2, 4, 80, 384), BF), vm((2, 8, 80, 384), BF),
            vm((2, 4, 80, 128), BF), vm((2, 4, 80, 128), BF),
            dma((2, 4)), dma((2, 4)), dma((2, 6)), dma((2, 6)), dma((2, 3)), dma((2, 3)),
            dma((2, 3)), dma((2, 3)), dma((2, 3)), dma((2, 3)), dma((2, 4)), dma((2, 8)),
            dma((2, 8)), dma((2, 4)),
        ],
        compiler_params=pltpu.CompilerParams(
            collective_id=0, has_side_effects=True, vmem_limit_bytes=LIMIT),
        name="block_pair",
    )(timestep, qkv_weight, proj_weight, time_table, block_tables, qk_gains, u, cotangent, *rope_arrays())


def hand_over_kernel(*refs):
    for source, target in zip(refs[:6], refs[6:]):
        target[...] = source[...]


def hand_over(arrays):
    return pl.pallas_call(
        hand_over_kernel, out_shape=tuple(sds(array.shape, array.dtype) for array in arrays),
        in_specs=[VM] * 6, out_specs=(VM,) * 6, name="hand_over",
    )(*arrays)


def local(tokens, timestep, time_table, block_tables, qk_gains, qkv_weight, proj_weight, cotangent):
    frame_dev, spatial, features = tokens.shape[1:]
    shape = (1, frame_dev, spatial, features)
    count = lax.axis_size("dp") * lax.axis_size("seq") * frame_dev * spatial
    block_out, token_grad, qkv_grad, proj_grad, table_grad, gain_grad = hand_over(block_pair(
        1.0 / math.sqrt(count), timestep, jnp.swapaxes(qkv_weight, 1, 2), jnp.swapaxes(proj_weight, 1, 2),
        jnp.swapaxes(time_table, 0, 1), jnp.swapaxes(block_tables, 0, 1), qk_gains,
        tokens.reshape(288, 1152), cotangent.reshape(288, 1152)))
    return (block_out.reshape(shape), token_grad.reshape(shape), jnp.swapaxes(qkv_grad, 0, 1),
            jnp.swapaxes(proj_grad, 0, 1), jnp.swapaxes(table_grad, 0, 1), gain_grad)


def solution(mesh):
    return jax.shard_map(
        local,
        mesh=mesh,
        in_specs=(
            PS("dp", "seq", None, None),
            PS("dp"),
            PS(),
            PS(),
            PS(),
            PS(),
            PS(),
            PS("dp", "seq", None, None),
        ),
        out_specs=(
            PS("dp", "seq", None, None),
            PS("dp", "seq", None, None),
            PS(None, "seq", "dp"),
            PS(None, "seq", "dp"),
            PS(),
            PS(),
        ),
        check_vma=False,
    )
```

```python
import math

import numpy as np
import jax
import jax.numpy as jnp
from jax import lax
from jax.experimental import pallas as pl
from jax.experimental.pallas import tpu as pltpu
from jax.sharding import PartitionSpec as PS

MESH = pl.DeviceIdType.MESH

HD = 72
EPS = 1e-06
F32 = jnp.float32
BF = jnp.bfloat16
SCALE = 1.0 / math.sqrt(HD)


def mm(a, b):
    return lax.dot_general(a, b, (((1,), (0,)), ((), ())), preferred_element_type=F32)


def mm_nt(a, b):
    return lax.dot_general(a, b, (((1,), (1,)), ((), ())), preferred_element_type=F32)


def mm_tn(a, b):
    return lax.dot_general(a, b, (((0,), (0,)), ((), ())), preferred_element_type=F32)


def row_norm(u):
    center = u - jnp.mean(u, -1, keepdims=True)
    inverse = lax.rsqrt(jnp.mean(center * center, -1, keepdims=True) + EPS)
    return center * inverse, inverse


def wide_gain(gain):
    none = jnp.zeros((1, 56), F32)
    return (jnp.concatenate([gain, none], 1),
            jnp.concatenate([gain[:, 36:72], gain[:, 0:36], none], 1))


def fill_grid(grid_ref):
    row = lax.broadcasted_iota(jnp.int32, (384, 256), 0) - 128
    column = lax.broadcasted_iota(jnp.int32, (384, 256), 1)
    second = column - 128
    partner = jnp.where(second < 36, second + 36, second - 36)
    wanted = jnp.where(column < 72, column,
                       jnp.where(jnp.logical_and(second >= 0, second < 72), partner, -1000))
    grid_ref[...] = jnp.where(row == wanted, 1.0, 0.0).astype(F32)


def placed(ref, index, grid_ref, width):
    start = 72 * index
    a = start // 128 * 128
    off = start - a
    size = 128 if off + 72 <= 128 else min(256, ref.shape[1] - a)
    return mm(ref[:, a:a + size], grid_ref[128 - off:128 - off + size, 0:width].astype(BF))


def unit_of(wide):
    factor = lax.rsqrt(jnp.sum(wide * wide, -1, keepdims=True) * (1.0 / HD) + EPS)
    return wide * factor, factor


def unit_back(grad, unit, factor):
    return factor * (grad - unit * (jnp.sum(grad * unit, -1, keepdims=True) * (1.0 / HD)))


def softmax(qh, kh):
    e = jnp.exp(mm_nt(qh, kh) * SCALE)
    return e / jnp.sum(e, -1, keepdims=True)


def modulation(ts_ref, time_ref, table_ref, mod_ref):
    chosen = lax.broadcasted_iota(jnp.int32, (16, 1152), 0) == ts_ref[0]
    for i in range(3):
        row = jnp.sum(jnp.where(chosen, time_ref[i], 0.0), 0, keepdims=True)
        for block in range(2):
            mod_ref[block, i:i + 1] = table_ref[i, block:block + 1] + row


def hidden_of(normed, mod_ref):
    return (normed * (1.0 + mod_ref[1:2]) + mod_ref[0:1]).astype(BF)


def spatial_forward(u, mod_ref, gain_ref, w_ref, wp_ref, loads, hid_ref, qkv_ref, heads_ref, att_ref, prob_ref,
                    grid_ref):
    normed, _ = row_norm(u)
    hid_ref[...] = hidden_of(normed, mod_ref)
    loads[0].wait()
    qkv_ref[...] = mm_nt(hid_ref[...], w_ref[...]).astype(BF)
    for i in range(24):
        heads_ref[i] = placed(qkv_ref, i, grid_ref, 128).astype(BF)
    gain_q, _ = wide_gain(gain_ref[0:1])
    gain_k, _ = wide_gain(gain_ref[1:2])
    parts = []
    for h in range(8):
        qh = (unit_of(heads_ref[h].astype(F32))[0] * gain_q).astype(BF)
        kh = (unit_of(heads_ref[8 + h].astype(F32))[0] * gain_k).astype(BF)
        v = heads_ref[16 + h]
        rows = []
        for g in range(3):
            s = slice(96 * g, 96 * g + 96)
            prob = softmax(qh[s], kh[s])
            prob_ref[3 * h + g] = prob
            rows.append(mm(prob.astype(BF), v[s]))
        parts.append(jnp.concatenate(rows, 0).astype(BF)[:, 0:72])
    att_ref[...] = jnp.concatenate(parts, 1)
    loads[1].wait()
    return (u + mod_ref[2:3] * mm(att_ref[...], wp_ref[...])).astype(BF)


class Heads:
    def __init__(self, probs, gain, rope, fetch, dat_ref, grid_ref):
        self.probs = probs
        forward = probs is None
        self.forward, self.rope, self.fetch, self.dat_ref, self.grid_ref = forward, rope, fetch, dat_ref, grid_ref
        self.att, self.back = [], ([], [], [])
        self.gain, partner = zip(wide_gain(gain[0:1]), wide_gain(gain[1:2]))
        if rope is not None:
            cosine, sine = rope
            self.turn = [(cosine * self.gain[i], sine * partner[i]) for i in range(2)]
            self.turn_back = (cosine * SCALE, sine * SCALE)
            self.swap = grid_ref[128:256, 128:256].astype(BF)
        self.gq = jnp.zeros((1, 128), F32)
        self.gk = jnp.zeros((1, 128), F32)

    def norm(self, index, which):
        raw = self.fetch(index)
        unit, factor = unit_of(raw[:, 0:128])
        if self.rope is None:
            half = (unit * self.gain[which]).astype(BF)
            return unit, factor, half, half
        straight, crossed = self.turn[which]
        half = (factor * (raw[:, 0:128] * straight + raw[:, 128:256] * crossed)).astype(BF)
        return unit, factor, half, jnp.concatenate([half, mm(half, self.swap).astype(BF)], 1)

    def back_turn(self, grads):
        grad = jnp.concatenate(grads, 0)
        if self.rope is None:
            return grad * SCALE
        return grad[:, 0:128] * self.turn_back[0] - grad[:, 128:256] * self.turn_back[1]

    def step(self, h):
        qu, qf, qh, qx = self.norm(h, 0)
        ku, kf, kh, kx = self.norm(8 + h, 1)
        v = self.fetch(16 + h)[:, 0:128].astype(BF)
        da = placed(self.dat_ref, h, self.grid_ref, 128).astype(BF)
        avs, dqs, dks, dvs = [], [], [], []
        for g in range(3):
            s = slice(96 * g, 96 * g + 96)
            att = softmax(qh[s], kh[s]) if self.forward else self.probs[3 * h + g]
            att16 = att.astype(BF)
            if self.forward:
                avs.append(mm(att16, v[s]))
            dp = mm_nt(da[s], v[s])
            dvs.append(mm_tn(att16, da[s]))
            ds = (att * (dp - jnp.sum(dp * att, -1, keepdims=True))).astype(BF)
            dqs.append(mm(ds, kx[s]))
            dks.append(mm_tn(ds, qx[s]))
        if self.forward:
            self.att.append(jnp.concatenate(avs, 0).astype(BF)[:, 0:72])
        dq = self.back_turn(dqs)
        dk = self.back_turn(dks)
        self.gq = self.gq + jnp.sum(dq * qu, 0, keepdims=True)
        self.gk = self.gk + jnp.sum(dk * ku, 0, keepdims=True)
        self.back[0].append(unit_back(dq * self.gain[0], qu, qf).astype(BF)[:, 0:72])
        self.back[1].append(unit_back(dk * self.gain[1], ku, kf).astype(BF)[:, 0:72])
        self.back[2].append(jnp.concatenate(dvs, 0).astype(BF)[:, 0:72])

    def qkv_back(self):
        return jnp.concatenate(self.back[0] + self.back[1] + self.back[2], 1)

    def gain_row(self):
        return jnp.concatenate([self.gq, self.gk, jnp.zeros((1, 1152 - 256), F32)], 1)


def after_heads(scale1, u_ref, g_ref, qkv_back, w_ref, grad_ref):
    hg = mm(qkv_back, w_ref[...])
    normed, inverse = row_norm(u_ref[...].astype(F32))
    ng = hg * scale1
    grad_ref[...] = (g_ref[...].astype(F32) + inverse * (
        ng - jnp.mean(ng, -1, keepdims=True)
        - normed * jnp.mean(ng * normed, -1, keepdims=True))).astype(BF)
    return hg, normed


def keep_terms(hg, normed, g_ref, projected, gain_row, stat_ref):
    stat_ref[...] = jnp.concatenate([
        jnp.sum(hg, 0, keepdims=True),
        jnp.sum(hg * normed, 0, keepdims=True),
        jnp.sum(g_ref[...].astype(F32) * projected, 0, keepdims=True),
        gain_row, jnp.zeros((4, 1152), F32)], 0)


def split_store(ref, value, width):
    ref[0] = value[:, 0:width]
    ref[1] = value[:, width:2 * width]


VM = pl.BlockSpec(memory_space=pltpu.VMEM)
HBM = pl.BlockSpec(memory_space=pl.ANY)
SMEM = pl.BlockSpec(memory_space=pltpu.SMEM)
LIMIT = 60 * 1024 * 1024


def sds(shape, dtype=BF):
    return jax.ShapeDtypeStruct(shape, dtype)


def rope_arrays():
    freq = np.power(10000.0, -2.0 * np.arange(36) / HD)
    angle = np.arange(96)[:, None] * freq[None]
    none = np.zeros((96, 56))
    cosine = np.concatenate([np.cos(angle), np.cos(angle), none], 1)
    sine = np.concatenate([-np.sin(angle), np.sin(angle), none], 1)
    return (jnp.asarray(np.tile(cosine, (3, 1)), F32), jnp.asarray(np.tile(sine, (3, 1)), F32))


def selector(rows, columns, place):
    at = lax.broadcasted_iota(jnp.int32, (rows, columns), 0)
    return jnp.where(lax.broadcasted_iota(jnp.int32, (rows, columns), 1) == place(at), 1.0, 0.0).astype(BF)


def fill_into(into_ref):
    def at(r, j):
        a = (r * 11) >> 5
        return 96 * a + 3 * j + r - 3 * a

    def into(test, shift):
        def find(i):
            r = i & 15
            return jnp.where(test(r), at(r - shift, i >> 4), -1)
        return find

    for k, (test, shift) in enumerate((
            (lambda r: r < 9, 0), (lambda r: r >= 9, 9),
            (lambda r: jnp.logical_or(r == 9, r == 10), 2),
            (lambda r: jnp.logical_or(r == 11, r == 12), 4))):
        into_ref[k] = selector(512, 288, into(test, shift))


def fill_back(from_ref):
    def back(low, shift):
        def find(o):
            b = (o >= 96).astype(jnp.int32) + (o >= 192).astype(jnp.int32)
            rest = o - 96 * b
            i = (rest * 683) >> 11
            r = 3 * (rest - 3 * i) + b
            place = 16 * i + r + shift
            if low is None:
                return place
            return jnp.where((r < 7) == low, place, -1)
        return find
    for k, (low, shift) in enumerate(((None, 0), (True, 9), (False, 2), (False, 4))):
        from_ref[k] = selector(288, 512, back(low, shift))


def pack(value, out_ref, into):
    tail = value[:, 768:1152]
    low = mm(into[0], value[:, 0:384]) + mm(into[1], tail)
    high = mm(into[0], value[:, 384:768]) + mm(into[2], tail)
    out_ref[:, :, 0:384] = low.astype(BF).reshape(32, 16, 384)
    out_ref[:, :, 384:768] = high.astype(BF).reshape(32, 16, 384)


def unpack(parcel_ref, back):
    low = parcel_ref[:, :, 0:384].reshape(512, 384)
    high = parcel_ref[:, :, 384:768].reshape(512, 384)
    tail = mm(back[1], low) + mm(back[2], high)
    return jnp.concatenate([mm(back[0], low), mm(back[0], high), tail], 1).astype(BF)


def pack_half(value, out_ref, into):
    tail = jnp.concatenate([value[:, 384:576], jnp.zeros((288, 64), BF)], 1)
    low = mm(into[0], value[:, 0:256]) + mm(into[1], tail)
    high = mm(into[0], value[:, 256:384]) + mm(into[2], tail[:, 0:128]) + mm(into[3], tail[:, 128:256])
    out_ref[:, :, 0:256] = low.astype(BF).reshape(32, 16, 256)
    out_ref[:, :, 256:384] = high.astype(BF).reshape(32, 16, 128)


def unpack_half(parcel_ref, back):
    low = parcel_ref[:, :, 0:256].reshape(512, 256)
    high = parcel_ref[:, :, 256:384].reshape(512, 128)
    tail = mm(back[1], low) + jnp.concatenate([mm(back[2], high), mm(back[3], high)], 1)
    return jnp.concatenate([mm(back[0], low), mm(back[0], high), tail[:, 0:192]], 1).astype(BF)


LA = 640
LB = 512


def place():
    dp = lax.axis_index("dp")
    seq = lax.axis_index("seq")
    return dp, seq, dp // 4, dp % 4, seq // 8, (seq // 2) % 4, seq % 2


def dev(dp, seq):
    return {"dp": dp, "seq": seq}


def remote(src, dst, send, recv, device):
    return pltpu.make_async_remote_copy(src_ref=src, dst_ref=dst, send_sem=send, recv_sem=recv,
                                        device_id=device, device_id_type=MESH)


class Sums:
    def __init__(self, sources, bufs, sems):
        self.hid, self.qkb, self.pin, self.att = sources
        (self.hid_s, self.qkb_s, self.pin_s, self.att_s, self.PA, self.PB, self.RA, self.RB, self.SA, self.SB,
         self.RA2, self.RB2, self.U, self.V, self.W, self.X) = bufs
        (self.act_send, self.act_recv, self.a_send, self.a_recv, self.b_send, self.b_recv, self.a2_send,
         self.a2_recv, self.b2_send, self.b2_recv, self.z_send, self.z_recv, self.f_send, self.f_recv) = sems
        self.dp, self.seq, self.z_hi, self.x, self.y, self.zl, self.c = place()
        self.z = self.z_hi * 4 + self.zl
        self.sib = self.y * 8 + self.zl * 2 + (1 - self.c)
        self.acts = {}

    def at_x(self, k):
        return dev(self.z_hi * 4 + (self.x + k) % 4, self.seq)

    def at_y(self, k):
        return dev(self.dp, ((self.y + k) % 4) * 8 + self.zl * 2 + self.c)

    def start_act(self, i):
        src, dst = ((self.hid, self.hid_s), (self.qkb.at[1 - self.c], self.qkb_s),
                    (self.pin, self.pin_s), (self.att.at[1 - self.c], self.att_s))[i]
        self.acts[i] = remote(src, dst, self.act_send.at[i], self.act_recv.at[i], dev(self.dp, self.sib))
        self.acts[i].start()

    def columns(self, left, left_s, right, right_s):
        for low, width in ((0, 256), (256, 256), (512, 128), (640, 256), (896, 256)):
            lanes = slice(low, low + width)
            yield low, width, mm_tn(left, right[:, lanes]) + mm_tn(left_s, right_s[:, lanes])

    def products_qkv(self):
        for act in (0, 1):
            self.acts[act].wait()
        PA, PB = self.PA, self.PB
        for low, width, acc in self.columns(self.qkb[self.c], self.qkb_s[...], self.hid, self.hid_s):
            if low < LA:
                for xo in range(4):
                    PA[xo, 0:216, low:low + width] = acc[216 * xo:216 * xo + 216].astype(BF)
            else:
                for q in range(3):
                    PB[q, :, low - LA:low - LA + width] = jnp.concatenate(
                        [acc[216 * xo + 72 * q:216 * xo + 72 * q + 72] for xo in range(4)], 0).astype(BF)
        self.ca, self.cb = [], []
        for k in range(1, 4):
            xx = (self.x + k) % 4
            yy = (self.y + k) % 4
            self.ca.append(remote(PA.at[xx, pl.ds(0, 208)], self.RA.at[k - 1, pl.ds(0, 208)],
                                  self.a_send.at[k - 1], self.a_recv.at[k - 1], self.at_x(k)))
            self.cb.append(remote(PB.at[yy], self.RB.at[k - 1], self.b_send.at[k - 1],
                                  self.b_recv.at[k - 1], self.at_y(k)))
        for k in range(3):
            self.ca[k].start()

            @pl.when((self.y + k + 1) % 4 != 3)
            def _(k=k):
                self.cb[k].start()

    def products_proj(self):
        for act in (2, 3):
            self.acts[act].wait()
        PA, PB = self.PA, self.PB
        for low, width, acc in self.columns(self.att[self.c], self.att_s[...], self.pin, self.pin_s):
            if low < LA:
                for xo in range(4):
                    PA[xo, 216:288, low:low + width] = acc[72 * xo:72 * xo + 72].astype(BF)
            else:
                PB[3, :, low - LA:low - LA + width] = acc.astype(BF)
        for k in range(1, 4):
            xx = (self.x + k) % 4
            self.ca.append(remote(PA.at[xx, pl.ds(208, 80)], self.RA.at[k - 1, pl.ds(208, 80)],
                                  self.a_send.at[k + 2], self.a_recv.at[k + 2], self.at_x(k)))
            self.ca[-1].start()

            @pl.when((self.y + k) % 4 == 3)
            def _(k=k):
                self.cb[k - 1].start()

    def add_up(self, own, others, into, width):
        def step(t, carry):
            lanes = pl.ds(pl.multiple_of(t * 128, 128), 128)
            tot = own[:, lanes].astype(F32)
            for k in range(3):
                tot = tot + others[k, :, lanes].astype(F32)
            for i in range(4):
                into[i, :, lanes] = jnp.concatenate(
                    [tot[72 * i:72 * i + 72], jnp.zeros((8, 128), F32)], 0).astype(BF)
            return carry
        lax.fori_loop(0, width // 128, step, 0)

    def first_sums(self):
        SA, SB, x, y = self.SA, self.SB, self.x, self.y
        for copy in self.cb:
            copy.wait()
        self.add_up(self.PB.at[y], self.RB, SB, LB)
        self.second = []
        for k in range(1, 4):
            self.second.append(remote(SB.at[(x + k) % 4], self.RB2.at[k - 1], self.b2_send.at[k - 1],
                                      self.b2_recv.at[k - 1], self.at_x(k)))
            self.second[-1].start()
        for copy in self.ca:
            copy.wait()

        self.add_up(self.PA.at[x], self.RA, SA, LA)
        for k in range(1, 4):
            self.second.append(remote(SA.at[(y + k) % 4], self.RA2.at[k - 1], self.a2_send.at[k - 1],
                                      self.a2_recv.at[k - 1], self.at_y(k)))
            self.second[-1].start()

    def second_sums(self):
        for copy in self.second:
            copy.wait()
        ta = self.SA[self.y].astype(F32)
        tb = self.SB[self.x].astype(F32)
        for k in range(3):
            ta = ta + self.RA2[k].astype(F32)
            tb = tb + self.RB2[k].astype(F32)
        full = jnp.concatenate([ta, tb], 1)
        for j in range(4):
            self.U[j] = jnp.concatenate(
                [full[:, 72 * (4 * yy + j): 72 * (4 * yy + j) + 72] for yy in range(4)]
                + [jnp.zeros((80, 96), F32)], 1).astype(BF)
        for j in range(4):
            copy = remote(self.U.at[j], self.V.at[self.z], self.z_send.at[j], self.z_recv.at[self.z],
                          dev(self.c * 4 + self.x, self.y * 8 + j * 2 + self.c))

            @pl.when(self.c * 4 + j != self.z)
            def _(copy=copy):
                copy.start()

    def z_sums(self):
        U, V, W, X, y, z = self.U, self.V, self.W, self.X, self.y, self.z

        @pl.when(self.z_hi == self.c)
        def _():
            V[z] = U[self.zl]
            for s in range(8):
                @pl.when(s != z)
                def _(s=s):
                    remote(U.at[0], V.at[s], self.z_send.at[0], self.z_recv.at[s],
                           dev(self.dp, self.seq)).wait_recv()
            tot = V[0].astype(F32)
            for s in range(1, 8):
                tot = tot + V[s].astype(F32)
            for i in range(4):
                W[i] = jnp.concatenate([tot[:, 72 * i: 72 * i + 72], jnp.zeros((80, 56), F32)],
                                       1).astype(BF)
            for yy in range(4):
                for cc in range(2):
                    mine = jnp.logical_and(yy == y, cc == self.c)

                    @pl.when(jnp.logical_not(mine))
                    def _(yy=yy, cc=cc):
                        remote(W.at[yy], X.at[y], self.f_send.at[yy * 2 + cc], self.f_recv.at[y],
                               dev(self.dp, yy * 8 + self.zl * 2 + cc)).start()

                    @pl.when(mine)
                    def _(yy=yy):
                        X[y] = W[yy]

    def finish(self, b, factor, qkv_out, proj_out):
        U, V, W, X, y, c = self.U, self.V, self.W, self.X, self.y, self.c
        for q in range(4):
            @pl.when(jnp.logical_not(jnp.logical_and(q == y, c == self.z_hi)))
            def _(q=q):
                remote(W.at[0], X.at[q], self.f_send.at[0], self.f_recv.at[q],
                       dev(self.dp, self.seq)).wait_recv()
        stacked = jnp.concatenate([X[q, 0:72, :].astype(F32) for q in range(4)], 0)
        turned = jnp.transpose(stacked, (1, 0)) * factor
        own = jnp.where(c == 0, turned[0:36], turned[36:72])
        qkv_out[:, b] = own[:, 0:216]
        proj_out[:, b] = own[:, 216:288]
        for j in range(4):
            @pl.when(c * 4 + j != self.z)
            def _(j=j):
                remote(U.at[j], V.at[0], self.z_send.at[j], self.z_recv.at[0],
                       dev(self.dp, self.seq)).wait_send()

        @pl.when(self.z_hi == c)
        def _():
            for yy in range(4):
                for cc in range(2):
                    @pl.when(jnp.logical_not(jnp.logical_and(yy == y, cc == c)))
                    def _(yy=yy, cc=cc):
                        remote(W.at[yy], X.at[0], self.f_send.at[yy * 2 + cc], self.f_recv.at[0],
                               dev(self.dp, self.seq)).wait_send()


class Terms:
    def __init__(self, T, levels, send, recv):
        self.T, self.levels, self.send, self.recv = T, levels, send, recv
        dp, seq, z_hi, x, y, zl, c = place()
        z = z_hi * 4 + zl
        self.me = (c, x, y, z)
        self.targets = (
            [dev(dp, y * 8 + zl * 2 + (1 - c))],
            [dev(z_hi * 4 + (x + k) % 4, seq) for k in range(1, 4)],
            [dev(dp, ((y + k) % 4) * 8 + zl * 2 + c) for k in range(1, 4)],
            [dev((((z + k) % 8) // 4) * 4 + x, y * 8 + ((z + k) % 4) * 2 + c) for k in range(1, 8)])

    def start(self, level):
        slots, me = self.levels[level], self.me[level]
        slots[me] = self.T[...]
        self.copies = [remote(self.T, slots.at[me], self.send.at[level, k], self.recv.at[level, k], target)
                       for k, target in enumerate(self.targets[level])]
        for copy in self.copies:
            copy.start()

    def end(self, level):
        for copy in self.copies:
            copy.wait()
        slots = self.levels[level]
        total = slots[0]
        for k in range(1, slots.shape[0]):
            total = total + slots[k]
        self.T[...] = total


def greet():
    dp, seq, z_hi, x, y, zl, c = place()
    barrier = pltpu.get_barrier_semaphore()
    peers = [dev(dp, (seq + k) % 32) for k in range(1, 32)]
    peers += [dev(z_hi * 4 + (x + k) % 4, seq) for k in range(1, 4)]
    peers += [dev((1 - z_hi) * 4 + x, y * 8 + k * 2 + c) for k in range(4)]
    for peer in peers:
        pl.semaphore_signal(barrier, inc=1, device_id=peer, device_id_type=MESH)
    return barrier, len(peers)


def exchange_start(parcel, landed, send, recv):
    dp = lax.axis_index("dp")
    seq = lax.axis_index("seq")
    copies = []
    for k in range(1, 32):
        to = (seq + k) % 32
        copies.append(remote(parcel.at[to], landed.at[seq], send.at[k], recv.at[k], dev(dp, to)))
        copies[-1].start()
    landed[seq] = parcel[seq]
    return copies


def pair_kernel(factor, ts_ref, w_hbm, wp_hbm, time_ref, table_ref, gains_ref, u_ref, cot_ref, cos_ref, sin_ref,
                out_ref, grad_ref, qkv_out, proj_out, table_out, gain_out, *scratch):
    (parcel, landed, halfp, half_landed, ex_send, ex_recv, into, back, mod_ref, qkv_ref, heads_ref, att_ref, prob_ref,
     u1_ref, mg_ref, dat_ref, hid, qkb, pin, att, stat, grid_ref, w_ref, wp_ref, w_sem,
     T, TC, TX, TY, TZ, t_send, t_recv) = scratch[:32]
    rest = scratch[32:]
    loads = []
    for block in range(2):
        loads.append([pltpu.make_async_copy(w_hbm.at[block], w_ref.at[block], w_sem.at[block, 0]),
                      pltpu.make_async_copy(wp_hbm.at[block], wp_ref.at[block], w_sem.at[block, 1])])
        for load in loads[-1]:
            load.start()
    barrier, count = greet()
    sums = [Sums([ref.at[b] for ref in (hid, qkb, pin, att)], [ref.at[b] for ref in rest[:16]],
                 [ref.at[b] for ref in rest[16:]]) for b in range(2)]
    early, late = sums
    terms = Terms(T, (TC, TX, TY, TZ), t_send, t_recv)
    fill_grid(grid_ref)
    fill_into(into)
    modulation(ts_ref, time_ref, table_ref, mod_ref)
    mods = [mod_ref.at[b] for b in range(2)]

    pack(spatial_forward(u_ref[...].astype(F32), mods[0], gains_ref.at[0], w_ref.at[0], wp_ref.at[0], loads[0],
                         hid.at[0], qkv_ref, heads_ref, att_ref, prob_ref, grid_ref), parcel, into)
    pl.semaphore_wait(barrier, count)
    moves = exchange_start(parcel, landed.at[0], ex_send.at[0], ex_recv.at[0])
    fill_back(back)
    split_store(att.at[0], att_ref[...], 288)
    early.start_act(0)
    early.start_act(3)
    gate = mods[1][2:3]
    pin[1] = (cot_ref[...].astype(F32) * gate).astype(BF)
    late.start_act(2)
    loads[1][1].wait()
    dat_ref[...] = mm_nt(pin[1], wp_ref[1]).astype(BF)
    for copy in moves:
        copy.wait()
    u1_ref[...] = unpack(landed.at[0], back)

    normed, _ = row_norm(u1_ref[...].astype(F32))
    hid[1] = hidden_of(normed, mods[1])
    late.start_act(0)
    loads[1][0].wait()
    qkv_ref[...] = mm_nt(hid[1], w_ref[1]).astype(BF)
    heads = Heads(None, gains_ref[1], (cos_ref[...], sin_ref[...]),
                  lambda i: placed(qkv_ref, i, grid_ref, 256 if i < 16 else 128), dat_ref, grid_ref)
    for h in range(8):
        heads.step(h)
    qkv_back = heads.qkv_back()
    attended = jnp.concatenate(heads.att, 1)
    split_store(qkb.at[1], qkv_back, 864)
    split_store(att.at[1], attended, 288)
    late.start_act(1)
    late.start_act(3)
    hg, normed = after_heads(1.0 + mods[1][1:2], u1_ref, cot_ref, qkv_back, w_ref.at[1], mg_ref)

    gate = mods[0][2:3]
    head_grad = mm_nt((mg_ref[...].astype(F32) * gate).astype(BF), wp_ref[0]).astype(BF)
    pack_half(head_grad, halfp, into)
    half_moves = exchange_start(halfp, half_landed, ex_send.at[1], ex_recv.at[1])
    pack(mg_ref[...], parcel, into)
    moves = exchange_start(parcel, landed.at[1], ex_send.at[2], ex_recv.at[2])
    late.products_qkv()
    late.products_proj()
    projected = mm(attended, wp_ref[1])
    out_ref[...] = (u1_ref[...].astype(F32) + mods[1][2:3] * projected).astype(BF)
    keep_terms(hg, normed, cot_ref, projected, heads.gain_row(), stat.at[1])
    for copy in half_moves:
        copy.wait()
    dat_ref[...] = unpack_half(half_landed, back)
    heads = Heads(prob_ref, gains_ref[0], None, lambda i: heads_ref[i].astype(F32), dat_ref, grid_ref)
    for h in range(8):
        heads.step(h)
    qkv_back = heads.qkv_back()
    split_store(qkb.at[0], qkv_back, 864)
    early.start_act(1)
    early.products_qkv()
    for copy in moves:
        copy.wait()
    u1_ref[...] = unpack(landed.at[1], back)
    pin[0] = (u1_ref[...].astype(F32) * gate).astype(BF)
    early.start_act(2)
    late.first_sums()
    early.products_proj()
    hg, normed = after_heads(1.0 + mods[0][1:2], u_ref, u1_ref, qkv_back, w_ref.at[0], grad_ref)
    keep_terms(hg, normed, u1_ref, mm(att_ref[...], wp_ref[0]), heads.gain_row(), stat.at[0])
    T[...] = jnp.concatenate([stat[0, 0:3], stat[1, 0:3], stat[0, 3:4], stat[1, 3:4]], 0)
    terms.start(0)
    late.second_sums()
    for level in range(3):
        terms.end(level)
        terms.start(level + 1)
    late.z_sums()
    early.first_sums()
    terms.end(3)
    total = T[...] * factor
    table_out[:, 0] = total[0:3]
    table_out[:, 1] = total[3:6]
    for b in range(2):
        gain_out[b] = jnp.concatenate([total[6 + b:7 + b, 0:72], total[6 + b:7 + b, 128:200]], 0)
    late.finish(1, factor, qkv_out, proj_out)
    early.second_sums()
    early.z_sums()
    early.finish(0, factor, qkv_out, proj_out)


def block_pair(factor, timestep, qkv_weight, proj_weight, time_table, block_tables, qk_gains, u, cotangent):
    dma = pltpu.SemaphoreType.DMA
    vm = pltpu.VMEM
    return pl.pallas_call(
        lambda *refs: pair_kernel(factor, *refs),
        out_shape=(sds((288, 1152)), sds((288, 1152)), sds((36, 2, 216), F32), sds((36, 2, 72), F32),
                   sds((3, 2, 1152), F32), sds((2, 2, 72), F32)),
        in_specs=[SMEM, HBM, HBM] + [VM] * 7, out_specs=(VM,) * 6,
        scratch_shapes=[
            vm((32, 16, 768), BF), vm((2, 32, 16, 768), BF), vm((32, 16, 384), BF), vm((32, 16, 384), BF),
            dma((3, 32)), dma((3, 32)), vm((4, 512, 288), BF), vm((4, 288, 512), BF), vm((2, 3, 1152), F32),
            vm((288, 1728), BF), vm((24, 288, 128), BF), vm((288, 576), BF), vm((24, 96, 96), F32),
            vm((288, 1152), BF), vm((288, 1152), BF), vm((288, 576), BF),
            vm((2, 288, 1152), BF), vm((2, 2, 288, 864), BF), vm((2, 288, 1152), BF), vm((2, 2, 288, 288), BF),
            vm((2, 8, 1152), F32), vm((384, 256), F32),
            vm((2, 1728, 1152), BF), vm((2, 576, 1152), BF), dma((2, 2)),
            vm((8, 1152), F32), vm((2, 8, 1152), F32), vm((4, 8, 1152), F32), vm((4, 8, 1152), F32),
            vm((8, 8, 1152), F32), dma((4, 7)), dma((4, 7)),
            vm((2, 288, 1152), BF), vm((2, 288, 864), BF), vm((2, 288, 1152), BF), vm((2, 288, 288), BF),
            vm((2, 4, 288, LA), BF), vm((2, 4, 288, LB), BF),
            vm((2, 3, 288, LA), BF), vm((2, 3, 288, LB), BF),
            vm((2, 4, 80, LA), BF), vm((2, 4, 80, LB), BF),
            vm((2, 3, 80, LA), BF), vm((2, 3, 80, LB), BF),
            vm((2, 4, 80, 384), BF), vm((2, 8, 80, 384), BF),
            vm((2, 4, 80, 128), BF), vm((2, 4, 80, 128), BF),
            dma((2, 4)), dma((2, 4)), dma((2, 6)), dma((2, 6)), dma((2, 3)), dma((2, 3)),
            dma((2, 3)), dma((2, 3)), dma((2, 3)), dma((2, 3)), dma((2, 4)), dma((2, 8)),
            dma((2, 8)), dma((2, 4)),
        ],
        compiler_params=pltpu.CompilerParams(
            collective_id=0, has_side_effects=True, vmem_limit_bytes=LIMIT),
        name="block_pair",
    )(timestep, qkv_weight, proj_weight, time_table, block_tables, qk_gains, u, cotangent, *rope_arrays())


def hand_over_kernel(*refs):
    for source, target in zip(refs[:6], refs[6:]):
        target[...] = source[...]


def hand_over(arrays):
    return pl.pallas_call(
        hand_over_kernel, out_shape=tuple(sds(array.shape, array.dtype) for array in arrays),
        in_specs=[VM] * 6, out_specs=(VM,) * 6, name="hand_over",
    )(*arrays)


def local(tokens, timestep, time_table, block_tables, qk_gains, qkv_weight, proj_weight, cotangent):
    frame_dev, spatial, features = tokens.shape[1:]
    shape = (1, frame_dev, spatial, features)
    count = lax.axis_size("dp") * lax.axis_size("seq") * frame_dev * spatial
    block_out, token_grad, qkv_grad, proj_grad, table_grad, gain_grad = hand_over(block_pair(
        1.0 / math.sqrt(count), timestep, jnp.swapaxes(qkv_weight, 1, 2), jnp.swapaxes(proj_weight, 1, 2),
        jnp.swapaxes(time_table, 0, 1), jnp.swapaxes(block_tables, 0, 1), qk_gains,
        tokens.reshape(288, 1152), cotangent.reshape(288, 1152)))
    return (block_out.reshape(shape), token_grad.reshape(shape), jnp.swapaxes(qkv_grad, 0, 1),
            jnp.swapaxes(proj_grad, 0, 1), jnp.swapaxes(table_grad, 0, 1), gain_grad)


def solution(mesh):
    return jax.shard_map(
        local,
        mesh=mesh,
        in_specs=(
            PS("dp", "seq", None, None),
            PS("dp"),
            PS(),
            PS(),
            PS(),
            PS(),
            PS(),
            PS("dp", "seq", None, None),
        ),
        out_specs=(
            PS("dp", "seq", None, None),
            PS("dp", "seq", None, None),
            PS(None, "seq", "dp"),
            PS(None, "seq", "dp"),
            PS(),
            PS(),
        ),
        check_vma=False,
    )
```

```python
import math

import numpy as np
import jax
import jax.numpy as jnp
from jax import lax
from jax.experimental import pallas as pl
from jax.experimental.pallas import tpu as pltpu
from jax.sharding import PartitionSpec as PS

MESH = pl.DeviceIdType.MESH

HD = 72
EPS = 1e-06
F32 = jnp.float32
BF = jnp.bfloat16
SCALE = 1.0 / math.sqrt(HD)


def mm(a, b):
    return lax.dot_general(a, b, (((1,), (0,)), ((), ())), preferred_element_type=F32)


def mm_nt(a, b):
    return lax.dot_general(a, b, (((1,), (1,)), ((), ())), preferred_element_type=F32)


def mm_tn(a, b):
    return lax.dot_general(a, b, (((0,), (0,)), ((), ())), preferred_element_type=F32)


def row_norm(u):
    center = u - jnp.mean(u, -1, keepdims=True)
    inverse = lax.rsqrt(jnp.mean(center * center, -1, keepdims=True) + EPS)
    return center * inverse, inverse


def wide_gain(gain):
    none = jnp.zeros((1, 56), F32)
    return (jnp.concatenate([gain, none], 1),
            jnp.concatenate([gain[:, 36:72], gain[:, 0:36], none], 1))


def fill_grid(grid_ref):
    row = lax.broadcasted_iota(jnp.int32, (384, 256), 0) - 128
    column = lax.broadcasted_iota(jnp.int32, (384, 256), 1)
    second = column - 128
    partner = jnp.where(second < 36, second + 36, second - 36)
    wanted = jnp.where(column < 72, column,
                       jnp.where(jnp.logical_and(second >= 0, second < 72), partner, -1000))
    grid_ref[...] = jnp.where(row == wanted, 1.0, 0.0).astype(F32)


def placed(ref, index, grid_ref, width):
    start = 72 * index
    a = start // 128 * 128
    off = start - a
    size = 128 if off + 72 <= 128 else min(256, ref.shape[1] - a)
    return mm(ref[:, a:a + size], grid_ref[128 - off:128 - off + size, 0:width].astype(BF))


def unit_of(wide):
    factor = lax.rsqrt(jnp.sum(wide * wide, -1, keepdims=True) * (1.0 / HD) + EPS)
    return wide * factor, factor


def unit_back(grad, unit, factor):
    return factor * (grad - unit * (jnp.sum(grad * unit, -1, keepdims=True) * (1.0 / HD)))


def softmax(qh, kh):
    e = jnp.exp(mm_nt(qh, kh) * SCALE)
    return e / jnp.sum(e, -1, keepdims=True)


def modulation(ts_ref, time_ref, table_ref, mod_ref):
    chosen = lax.broadcasted_iota(jnp.int32, (16, 1152), 0) == ts_ref[0]
    for i in range(3):
        row = jnp.sum(jnp.where(chosen, time_ref[i], 0.0), 0, keepdims=True)
        for block in range(2):
            mod_ref[block, i:i + 1] = table_ref[i, block:block + 1] + row


def hidden_of(normed, mod_ref):
    return (normed * (1.0 + mod_ref[1:2]) + mod_ref[0:1]).astype(BF)


def spatial_forward(u, mod_ref, gain_ref, w_ref, wp_ref, loads, hid_ref, qkv_ref, heads_ref, att_ref, prob_ref,
                    grid_ref):
    normed, _ = row_norm(u)
    hid_ref[...] = hidden_of(normed, mod_ref)
    loads[0].wait()
    qkv_ref[...] = mm_nt(hid_ref[...], w_ref[...]).astype(BF)
    for i in range(24):
        heads_ref[i] = placed(qkv_ref, i, grid_ref, 128).astype(BF)
    gain_q, _ = wide_gain(gain_ref[0:1])
    gain_k, _ = wide_gain(gain_ref[1:2])
    parts = []
    for h in range(8):
        qh = (unit_of(heads_ref[h].astype(F32))[0] * gain_q).astype(BF)
        kh = (unit_of(heads_ref[8 + h].astype(F32))[0] * gain_k).astype(BF)
        v = heads_ref[16 + h]
        rows = []
        for g in range(3):
            s = slice(96 * g, 96 * g + 96)
            prob = softmax(qh[s], kh[s])
            prob_ref[3 * h + g] = prob
            rows.append(mm(prob.astype(BF), v[s]))
        parts.append(jnp.concatenate(rows, 0).astype(BF)[:, 0:72])
    att_ref[...] = jnp.concatenate(parts, 1)
    loads[1].wait()
    return (u + mod_ref[2:3] * mm(att_ref[...], wp_ref[...])).astype(BF)


class Heads:
    def __init__(self, probs, gain, rope, fetch, dat_ref, grid_ref):
        self.probs = probs
        forward = probs is None
        self.forward, self.rope, self.fetch, self.dat_ref, self.grid_ref = forward, rope, fetch, dat_ref, grid_ref
        self.att, self.back = [], ([], [], [])
        self.gain, partner = zip(wide_gain(gain[0:1]), wide_gain(gain[1:2]))
        if rope is not None:
            cosine, sine = rope
            self.turn = [(cosine * self.gain[i], sine * partner[i]) for i in range(2)]
            self.turn_back = (cosine * SCALE, sine * SCALE)
            self.swap = grid_ref[128:256, 128:256].astype(BF)
        self.gq = jnp.zeros((1, 128), F32)
        self.gk = jnp.zeros((1, 128), F32)

    def norm(self, index, which):
        raw = self.fetch(index)
        unit, factor = unit_of(raw[:, 0:128])
        if self.rope is None:
            half = (unit * self.gain[which]).astype(BF)
            return unit, factor, half, half
        straight, crossed = self.turn[which]
        half = (factor * (raw[:, 0:128] * straight + raw[:, 128:256] * crossed)).astype(BF)
        return unit, factor, half, jnp.concatenate([half, mm(half, self.swap).astype(BF)], 1)

    def back_turn(self, grads):
        grad = jnp.concatenate(grads, 0)
        if self.rope is None:
            return grad * SCALE
        return grad[:, 0:128] * self.turn_back[0] - grad[:, 128:256] * self.turn_back[1]

    def step(self, h):
        qu, qf, qh, qx = self.norm(h, 0)
        ku, kf, kh, kx = self.norm(8 + h, 1)
        v = self.fetch(16 + h)[:, 0:128].astype(BF)
        da = placed(self.dat_ref, h, self.grid_ref, 128).astype(BF)
        avs, dqs, dks, dvs = [], [], [], []
        for g in range(3):
            s = slice(96 * g, 96 * g + 96)
            att = softmax(qh[s], kh[s]) if self.forward else self.probs[3 * h + g]
            att16 = att.astype(BF)
            if self.forward:
                avs.append(mm(att16, v[s]))
            dp = mm_nt(da[s], v[s])
            dvs.append(mm_tn(att16, da[s]))
            ds = (att * (dp - jnp.sum(dp * att, -1, keepdims=True))).astype(BF)
            dqs.append(mm(ds, kx[s]))
            dks.append(mm_tn(ds, qx[s]))
        if self.forward:
            self.att.append(jnp.concatenate(avs, 0).astype(BF)[:, 0:72])
        dq = self.back_turn(dqs)
        dk = self.back_turn(dks)
        self.gq = self.gq + jnp.sum(dq * qu, 0, keepdims=True)
        self.gk = self.gk + jnp.sum(dk * ku, 0, keepdims=True)
        self.back[0].append(unit_back(dq * self.gain[0], qu, qf).astype(BF)[:, 0:72])
        self.back[1].append(unit_back(dk * self.gain[1], ku, kf).astype(BF)[:, 0:72])
        self.back[2].append(jnp.concatenate(dvs, 0).astype(BF)[:, 0:72])

    def qkv_back(self):
        return jnp.concatenate(self.back[0] + self.back[1] + self.back[2], 1)

    def gain_row(self):
        return jnp.concatenate([self.gq, self.gk, jnp.zeros((1, 1152 - 256), F32)], 1)


def after_heads(scale1, u_ref, g_ref, qkv_back, w_ref, grad_ref):
    hg = mm(qkv_back, w_ref[...])
    normed, inverse = row_norm(u_ref[...].astype(F32))
    ng = hg * scale1
    grad_ref[...] = (g_ref[...].astype(F32) + inverse * (
        ng - jnp.mean(ng, -1, keepdims=True)
        - normed * jnp.mean(ng * normed, -1, keepdims=True))).astype(BF)
    return hg, normed


def keep_terms(hg, normed, g_ref, projected, gain_row, stat_ref):
    stat_ref[...] = jnp.concatenate([
        jnp.sum(hg, 0, keepdims=True),
        jnp.sum(hg * normed, 0, keepdims=True),
        jnp.sum(g_ref[...].astype(F32) * projected, 0, keepdims=True),
        gain_row, jnp.zeros((4, 1152), F32)], 0)


def split_store(ref, value, width):
    ref[0] = value[:, 0:width]
    ref[1] = value[:, width:2 * width]


VM = pl.BlockSpec(memory_space=pltpu.VMEM)
HBM = pl.BlockSpec(memory_space=pl.ANY)
SMEM = pl.BlockSpec(memory_space=pltpu.SMEM)
LIMIT = 60 * 1024 * 1024


def sds(shape, dtype=BF):
    return jax.ShapeDtypeStruct(shape, dtype)


def rope_arrays():
    freq = np.power(10000.0, -2.0 * np.arange(36) / HD)
    angle = np.arange(96)[:, None] * freq[None]
    none = np.zeros((96, 56))
    cosine = np.concatenate([np.cos(angle), np.cos(angle), none], 1)
    sine = np.concatenate([-np.sin(angle), np.sin(angle), none], 1)
    return (jnp.asarray(np.tile(cosine, (3, 1)), F32), jnp.asarray(np.tile(sine, (3, 1)), F32))


def selector(rows, columns, place):
    at = lax.broadcasted_iota(jnp.int32, (rows, columns), 0)
    return jnp.where(lax.broadcasted_iota(jnp.int32, (rows, columns), 1) == place(at), 1.0, 0.0).astype(BF)


def fill_into(into_ref):
    def at(r, j):
        a = (r * 11) >> 5
        return 96 * a + 3 * j + r - 3 * a

    def into(test, shift):
        def find(i):
            r = i & 15
            return jnp.where(test(r), at(r - shift, i >> 4), -1)
        return find

    for k, (test, shift) in enumerate((
            (lambda r: r < 9, 0), (lambda r: r >= 9, 9),
            (lambda r: jnp.logical_or(r == 9, r == 10), 2),
            (lambda r: jnp.logical_or(r == 11, r == 12), 4))):
        into_ref[k] = selector(512, 288, into(test, shift))


def fill_back(from_ref):
    def back(low, shift):
        def find(o):
            b = (o >= 96).astype(jnp.int32) + (o >= 192).astype(jnp.int32)
            rest = o - 96 * b
            i = (rest * 683) >> 11
            r = 3 * (rest - 3 * i) + b
            place = 16 * i + r + shift
            if low is None:
                return place
            return jnp.where((r < 7) == low, place, -1)
        return find
    for k, (low, shift) in enumerate(((None, 0), (True, 9), (False, 2), (False, 4))):
        from_ref[k] = selector(288, 512, back(low, shift))


def pack(value, out_ref, into):
    tail = value[:, 768:1152]
    low = mm(into[0], value[:, 0:384]) + mm(into[1], tail)
    high = mm(into[0], value[:, 384:768]) + mm(into[2], tail)
    out_ref[:, :, 0:384] = low.astype(BF).reshape(32, 16, 384)
    out_ref[:, :, 384:768] = high.astype(BF).reshape(32, 16, 384)


def unpack(parcel_ref, back):
    low = parcel_ref[:, :, 0:384].reshape(512, 384)
    high = parcel_ref[:, :, 384:768].reshape(512, 384)
    tail = mm(back[1], low) + mm(back[2], high)
    return jnp.concatenate([mm(back[0], low), mm(back[0], high), tail], 1).astype(BF)


def pack_half(value, out_ref, into):
    tail = jnp.concatenate([value[:, 384:576], jnp.zeros((288, 64), BF)], 1)
    low = mm(into[0], value[:, 0:256]) + mm(into[1], tail)
    high = mm(into[0], value[:, 256:384]) + mm(into[2], tail[:, 0:128]) + mm(into[3], tail[:, 128:256])
    out_ref[:, :, 0:256] = low.astype(BF).reshape(32, 16, 256)
    out_ref[:, :, 256:384] = high.astype(BF).reshape(32, 16, 128)


def unpack_half(parcel_ref, back):
    low = parcel_ref[:, :, 0:256].reshape(512, 256)
    high = parcel_ref[:, :, 256:384].reshape(512, 128)
    tail = mm(back[1], low) + jnp.concatenate([mm(back[2], high), mm(back[3], high)], 1)
    return jnp.concatenate([mm(back[0], low), mm(back[0], high), tail[:, 0:192]], 1).astype(BF)


LA = 640
LB = 512


def place():
    dp = lax.axis_index("dp")
    seq = lax.axis_index("seq")
    return dp, seq, dp // 4, dp % 4, seq // 8, (seq // 2) % 4, seq % 2


def dev(dp, seq):
    return {"dp": dp, "seq": seq}


def remote(src, dst, send, recv, device):
    return pltpu.make_async_remote_copy(src_ref=src, dst_ref=dst, send_sem=send, recv_sem=recv,
                                        device_id=device, device_id_type=MESH)


class Sums:
    def __init__(self, sources, bufs, sems):
        self.hid, self.qkb, self.pin, self.att = sources
        (self.hid_s, self.qkb_s, self.pin_s, self.att_s, self.PA, self.PB, self.RA, self.RB, self.SA, self.SB,
         self.RA2, self.RB2, self.U, self.V, self.W, self.X) = bufs
        (self.act_send, self.act_recv, self.a_send, self.a_recv, self.b_send, self.b_recv, self.a2_send,
         self.a2_recv, self.b2_send, self.b2_recv, self.z_send, self.z_recv, self.f_send, self.f_recv) = sems
        self.dp, self.seq, self.z_hi, self.x, self.y, self.zl, self.c = place()
        self.z = self.z_hi * 4 + self.zl
        self.sib = self.y * 8 + self.zl * 2 + (1 - self.c)
        self.acts = {}

    def at_x(self, k):
        return dev(self.z_hi * 4 + (self.x + k) % 4, self.seq)

    def at_y(self, k):
        return dev(self.dp, ((self.y + k) % 4) * 8 + self.zl * 2 + self.c)

    def start_act(self, i):
        src, dst = ((self.hid, self.hid_s), (self.qkb.at[1 - self.c], self.qkb_s),
                    (self.pin, self.pin_s), (self.att.at[1 - self.c], self.att_s))[i]
        self.acts[i] = remote(src, dst, self.act_send.at[i], self.act_recv.at[i], dev(self.dp, self.sib))
        self.acts[i].start()

    def columns(self, left, left_s, right, right_s):
        for low, width in ((0, 256), (256, 256), (512, 128), (640, 256), (896, 256)):
            lanes = slice(low, low + width)
            yield low, width, mm_tn(left, right[:, lanes]) + mm_tn(left_s, right_s[:, lanes])

    def products_qkv(self):
        for act in (0, 1):
            self.acts[act].wait()
        PA, PB = self.PA, self.PB
        for low, width, acc in self.columns(self.qkb[self.c], self.qkb_s[...], self.hid, self.hid_s):
            if low < LA:
                for xo in range(4):
                    PA[xo, 0:216, low:low + width] = acc[216 * xo:216 * xo + 216].astype(BF)
            else:
                for q in range(3):
                    PB[q, :, low - LA:low - LA + width] = jnp.concatenate(
                        [acc[216 * xo + 72 * q:216 * xo + 72 * q + 72] for xo in range(4)], 0).astype(BF)
        self.ca, self.cb = [], []
        for k in range(1, 4):
            xx = (self.x + k) % 4
            yy = (self.y + k) % 4
            self.ca.append(remote(PA.at[xx, pl.ds(0, 208)], self.RA.at[k - 1, pl.ds(0, 208)],
                                  self.a_send.at[k - 1], self.a_recv.at[k - 1], self.at_x(k)))
            self.cb.append(remote(PB.at[yy], self.RB.at[k - 1], self.b_send.at[k - 1],
                                  self.b_recv.at[k - 1], self.at_y(k)))
        for k in range(3):
            self.ca[k].start()

            @pl.when((self.y + k + 1) % 4 != 3)
            def _(k=k):
                self.cb[k].start()

    def products_proj(self):
        for act in (2, 3):
            self.acts[act].wait()
        PA, PB = self.PA, self.PB
        for low, width, acc in self.columns(self.att[self.c], self.att_s[...], self.pin, self.pin_s):
            if low < LA:
                for xo in range(4):
                    PA[xo, 216:288, low:low + width] = acc[72 * xo:72 * xo + 72].astype(BF)
            else:
                PB[3, :, low - LA:low - LA + width] = acc.astype(BF)
        for k in range(1, 4):
            xx = (self.x + k) % 4
            self.ca.append(remote(PA.at[xx, pl.ds(208, 80)], self.RA.at[k - 1, pl.ds(208, 80)],
                                  self.a_send.at[k + 2], self.a_recv.at[k + 2], self.at_x(k)))
            self.ca[-1].start()

            @pl.when((self.y + k) % 4 == 3)
            def _(k=k):
                self.cb[k - 1].start()

    def add_up(self, own, others, into, width):
        def step(t, carry):
            lanes = pl.ds(pl.multiple_of(t * 128, 128), 128)
            tot = own[:, lanes].astype(F32)
            for k in range(3):
                tot = tot + others[k, :, lanes].astype(F32)
            for i in range(4):
                into[i, :, lanes] = jnp.concatenate(
                    [tot[72 * i:72 * i + 72], jnp.zeros((8, 128), F32)], 0).astype(BF)
            return carry
        lax.fori_loop(0, width // 128, step, 0)

    def first_sums(self):
        SA, SB, x, y = self.SA, self.SB, self.x, self.y
        for copy in self.cb:
            copy.wait()
        self.add_up(self.PB.at[y], self.RB, SB, LB)
        self.second = []
        for k in range(1, 4):
            self.second.append(remote(SB.at[(x + k) % 4], self.RB2.at[k - 1], self.b2_send.at[k - 1],
                                      self.b2_recv.at[k - 1], self.at_x(k)))
            self.second[-1].start()
        for copy in self.ca:
            copy.wait()

        self.add_up(self.PA.at[x], self.RA, SA, LA)
        for k in range(1, 4):
            self.second.append(remote(SA.at[(y + k) % 4], self.RA2.at[k - 1], self.a2_send.at[k - 1],
                                      self.a2_recv.at[k - 1], self.at_y(k)))
            self.second[-1].start()

    def second_sums(self):
        for copy in self.second:
            copy.wait()
        ta = self.SA[self.y].astype(F32)
        tb = self.SB[self.x].astype(F32)
        for k in range(3):
            ta = ta + self.RA2[k].astype(F32)
            tb = tb + self.RB2[k].astype(F32)
        full = jnp.concatenate([ta, tb], 1)
        for j in range(4):
            self.U[j] = jnp.concatenate(
                [full[:, 72 * (4 * yy + j): 72 * (4 * yy + j) + 72] for yy in range(4)]
                + [jnp.zeros((80, 96), F32)], 1).astype(BF)
        for j in range(4):
            copy = remote(self.U.at[j], self.V.at[self.z], self.z_send.at[j], self.z_recv.at[self.z],
                          dev(self.c * 4 + self.x, self.y * 8 + j * 2 + self.c))

            @pl.when(self.c * 4 + j != self.z)
            def _(copy=copy):
                copy.start()

    def z_sums(self):
        U, V, W, X, y, z = self.U, self.V, self.W, self.X, self.y, self.z

        @pl.when(self.z_hi == self.c)
        def _():
            V[z] = U[self.zl]
            for s in range(8):
                @pl.when(s != z)
                def _(s=s):
                    remote(U.at[0], V.at[s], self.z_send.at[0], self.z_recv.at[s],
                           dev(self.dp, self.seq)).wait_recv()
            tot = V[0].astype(F32)
            for s in range(1, 8):
                tot = tot + V[s].astype(F32)
            for i in range(4):
                W[i] = jnp.concatenate([tot[:, 72 * i: 72 * i + 72], jnp.zeros((80, 56), F32)],
                                       1).astype(BF)
            for yy in range(4):
                for cc in range(2):
                    mine = jnp.logical_and(yy == y, cc == self.c)

                    @pl.when(jnp.logical_not(mine))
                    def _(yy=yy, cc=cc):
                        remote(W.at[yy], X.at[y], self.f_send.at[yy * 2 + cc], self.f_recv.at[y],
                               dev(self.dp, yy * 8 + self.zl * 2 + cc)).start()

                    @pl.when(mine)
                    def _(yy=yy):
                        X[y] = W[yy]

    def finish(self, b, factor, qkv_out, proj_out):
        U, V, W, X, y, c = self.U, self.V, self.W, self.X, self.y, self.c
        for q in range(4):
            @pl.when(jnp.logical_not(jnp.logical_and(q == y, c == self.z_hi)))
            def _(q=q):
                remote(W.at[0], X.at[q], self.f_send.at[0], self.f_recv.at[q],
                       dev(self.dp, self.seq)).wait_recv()
        stacked = jnp.concatenate([X[q, 0:72, :].astype(F32) for q in range(4)], 0)
        turned = jnp.transpose(stacked, (1, 0)) * factor
        own = jnp.where(c == 0, turned[0:36], turned[36:72])
        qkv_out[:, b] = own[:, 0:216]
        proj_out[:, b] = own[:, 216:288]
        for j in range(4):
            @pl.when(c * 4 + j != self.z)
            def _(j=j):
                remote(U.at[j], V.at[0], self.z_send.at[j], self.z_recv.at[0],
                       dev(self.dp, self.seq)).wait_send()

        @pl.when(self.z_hi == c)
        def _():
            for yy in range(4):
                for cc in range(2):
                    @pl.when(jnp.logical_not(jnp.logical_and(yy == y, cc == c)))
                    def _(yy=yy, cc=cc):
                        remote(W.at[yy], X.at[0], self.f_send.at[yy * 2 + cc], self.f_recv.at[0],
                               dev(self.dp, self.seq)).wait_send()


class Terms:
    def __init__(self, T, levels, send, recv):
        self.T, self.levels, self.send, self.recv = T, levels, send, recv
        dp, seq, z_hi, x, y, zl, c = place()
        z = z_hi * 4 + zl
        self.me = (c, x, y, z)
        self.targets = (
            [dev(dp, y * 8 + zl * 2 + (1 - c))],
            [dev(z_hi * 4 + (x + k) % 4, seq) for k in range(1, 4)],
            [dev(dp, ((y + k) % 4) * 8 + zl * 2 + c) for k in range(1, 4)],
            [dev((((z + k) % 8) // 4) * 4 + x, y * 8 + ((z + k) % 4) * 2 + c) for k in range(1, 8)])

    def start(self, level):
        slots, me = self.levels[level], self.me[level]
        slots[me] = self.T[...]
        self.copies = [remote(self.T, slots.at[me], self.send.at[level, k], self.recv.at[level, k], target)
                       for k, target in enumerate(self.targets[level])]
        for copy in self.copies:
            copy.start()

    def end(self, level):
        for copy in self.copies:
            copy.wait()
        slots = self.levels[level]
        total = slots[0]
        for k in range(1, slots.shape[0]):
            total = total + slots[k]
        self.T[...] = total


def greet():
    dp, seq, z_hi, x, y, zl, c = place()
    barrier = pltpu.get_barrier_semaphore()
    peers = [dev(dp, (seq + k) % 32) for k in range(1, 32)]
    peers += [dev(z_hi * 4 + (x + k) % 4, seq) for k in range(1, 4)]
    peers += [dev((1 - z_hi) * 4 + x, y * 8 + k * 2 + c) for k in range(4)]
    for peer in peers:
        pl.semaphore_signal(barrier, inc=1, device_id=peer, device_id_type=MESH)
    return barrier, len(peers)


def exchange_start(parcel, landed, send, recv):
    dp = lax.axis_index("dp")
    seq = lax.axis_index("seq")
    copies = []
    for k in range(1, 32):
        to = (seq + k) % 32
        copies.append(remote(parcel.at[to], landed.at[seq], send.at[k], recv.at[k], dev(dp, to)))
        copies[-1].start()
    landed[seq] = parcel[seq]
    return copies


def pair_kernel(factor, ts_ref, w_hbm, wp_hbm, time_ref, table_ref, gains_ref, u_ref, cot_ref, cos_ref, sin_ref,
                out_ref, grad_ref, qkv_out, proj_out, table_out, gain_out, *scratch):
    (parcel, landed, halfp, half_landed, ex_send, ex_recv, into, back, mod_ref, qkv_ref, heads_ref, att_ref, prob_ref,
     u1_ref, mg_ref, dat_ref, hid, qkb, pin, att, stat, grid_ref, w_ref, wp_ref, w_sem,
     T, TC, TX, TY, TZ, t_send, t_recv) = scratch[:32]
    rest = scratch[32:]
    loads = []
    for block in range(2):
        loads.append([pltpu.make_async_copy(w_hbm.at[block], w_ref.at[block], w_sem.at[block, 0]),
                      pltpu.make_async_copy(wp_hbm.at[block], wp_ref.at[block], w_sem.at[block, 1])])
        for load in loads[-1]:
            load.start()
    barrier, count = greet()
    sums = [Sums([ref.at[b] for ref in (hid, qkb, pin, att)], [ref.at[b] for ref in rest[:16]],
                 [ref.at[b] for ref in rest[16:]]) for b in range(2)]
    early, late = sums
    terms = Terms(T, (TC, TX, TY, TZ), t_send, t_recv)
    fill_grid(grid_ref)
    fill_into(into)
    modulation(ts_ref, time_ref, table_ref, mod_ref)
    mods = [mod_ref.at[b] for b in range(2)]

    pack(spatial_forward(u_ref[...].astype(F32), mods[0], gains_ref.at[0], w_ref.at[0], wp_ref.at[0], loads[0],
                         hid.at[0], qkv_ref, heads_ref, att_ref, prob_ref, grid_ref), parcel, into)
    pl.semaphore_wait(barrier, count)
    moves = exchange_start(parcel, landed.at[0], ex_send.at[0], ex_recv.at[0])
    fill_back(back)
    split_store(att.at[0], att_ref[...], 288)
    early.start_act(0)
    early.start_act(3)
    gate = mods[1][2:3]
    pin[1] = (cot_ref[...].astype(F32) * gate).astype(BF)
    late.start_act(2)
    loads[1][1].wait()
    dat_ref[...] = mm_nt(pin[1], wp_ref[1]).astype(BF)
    for copy in moves:
        copy.wait()
    u1_ref[...] = unpack(landed.at[0], back)

    normed, _ = row_norm(u1_ref[...].astype(F32))
    hid[1] = hidden_of(normed, mods[1])
    late.start_act(0)
    loads[1][0].wait()
    qkv_ref[...] = mm_nt(hid[1], w_ref[1]).astype(BF)
    heads = Heads(None, gains_ref[1], (cos_ref[...], sin_ref[...]),
                  lambda i: placed(qkv_ref, i, grid_ref, 256 if i < 16 else 128), dat_ref, grid_ref)
    for h in range(8):
        heads.step(h)
    qkv_back = heads.qkv_back()
    attended = jnp.concatenate(heads.att, 1)
    split_store(qkb.at[1], qkv_back, 864)
    split_store(att.at[1], attended, 288)
    late.start_act(1)
    late.start_act(3)
    hg, normed = after_heads(1.0 + mods[1][1:2], u1_ref, cot_ref, qkv_back, w_ref.at[1], mg_ref)

    gate = mods[0][2:3]
    head_grad = mm_nt((mg_ref[...].astype(F32) * gate).astype(BF), wp_ref[0]).astype(BF)
    pack_half(head_grad, halfp, into)
    half_moves = exchange_start(halfp, half_landed, ex_send.at[1], ex_recv.at[1])
    pack(mg_ref[...], parcel, into)
    late.products_qkv()
    late.products_proj()
    moves = exchange_start(parcel, landed.at[1], ex_send.at[2], ex_recv.at[2])
    projected = mm(attended, wp_ref[1])
    out_ref[...] = (u1_ref[...].astype(F32) + mods[1][2:3] * projected).astype(BF)
    keep_terms(hg, normed, cot_ref, projected, heads.gain_row(), stat.at[1])
    for copy in half_moves:
        copy.wait()
    dat_ref[...] = unpack_half(half_landed, back)
    heads = Heads(prob_ref, gains_ref[0], None, lambda i: heads_ref[i].astype(F32), dat_ref, grid_ref)
    for h in range(8):
        heads.step(h)
    qkv_back = heads.qkv_back()
    split_store(qkb.at[0], qkv_back, 864)
    early.start_act(1)
    early.products_qkv()
    for copy in moves:
        copy.wait()
    u1_ref[...] = unpack(landed.at[1], back)
    pin[0] = (u1_ref[...].astype(F32) * gate).astype(BF)
    early.start_act(2)
    late.first_sums()
    early.products_proj()
    hg, normed = after_heads(1.0 + mods[0][1:2], u_ref, u1_ref, qkv_back, w_ref.at[0], grad_ref)
    keep_terms(hg, normed, u1_ref, mm(att_ref[...], wp_ref[0]), heads.gain_row(), stat.at[0])
    T[...] = jnp.concatenate([stat[0, 0:3], stat[1, 0:3], stat[0, 3:4], stat[1, 3:4]], 0)
    terms.start(0)
    late.second_sums()
    for level in range(3):
        terms.end(level)
        terms.start(level + 1)
    late.z_sums()
    early.first_sums()
    terms.end(3)
    total = T[...] * factor
    table_out[:, 0] = total[0:3]
    table_out[:, 1] = total[3:6]
    for b in range(2):
        gain_out[b] = jnp.concatenate([total[6 + b:7 + b, 0:72], total[6 + b:7 + b, 128:200]], 0)
    late.finish(1, factor, qkv_out, proj_out)
    early.second_sums()
    early.z_sums()
    early.finish(0, factor, qkv_out, proj_out)


def block_pair(factor, timestep, qkv_weight, proj_weight, time_table, block_tables, qk_gains, u, cotangent):
    dma = pltpu.SemaphoreType.DMA
    vm = pltpu.VMEM
    return pl.pallas_call(
        lambda *refs: pair_kernel(factor, *refs),
        out_shape=(sds((288, 1152)), sds((288, 1152)), sds((36, 2, 216), F32), sds((36, 2, 72), F32),
                   sds((3, 2, 1152), F32), sds((2, 2, 72), F32)),
        in_specs=[SMEM, HBM, HBM] + [VM] * 7, out_specs=(VM,) * 6,
        scratch_shapes=[
            vm((32, 16, 768), BF), vm((2, 32, 16, 768), BF), vm((32, 16, 384), BF), vm((32, 16, 384), BF),
            dma((3, 32)), dma((3, 32)), vm((4, 512, 288), BF), vm((4, 288, 512), BF), vm((2, 3, 1152), F32),
            vm((288, 1728), BF), vm((24, 288, 128), BF), vm((288, 576), BF), vm((24, 96, 96), F32),
            vm((288, 1152), BF), vm((288, 1152), BF), vm((288, 576), BF),
            vm((2, 288, 1152), BF), vm((2, 2, 288, 864), BF), vm((2, 288, 1152), BF), vm((2, 2, 288, 288), BF),
            vm((2, 8, 1152), F32), vm((384, 256), F32),
            vm((2, 1728, 1152), BF), vm((2, 576, 1152), BF), dma((2, 2)),
            vm((8, 1152), F32), vm((2, 8, 1152), F32), vm((4, 8, 1152), F32), vm((4, 8, 1152), F32),
            vm((8, 8, 1152), F32), dma((4, 7)), dma((4, 7)),
            vm((2, 288, 1152), BF), vm((2, 288, 864), BF), vm((2, 288, 1152), BF), vm((2, 288, 288), BF),
            vm((2, 4, 288, LA), BF), vm((2, 4, 288, LB), BF),
            vm((2, 3, 288, LA), BF), vm((2, 3, 288, LB), BF),
            vm((2, 4, 80, LA), BF), vm((2, 4, 80, LB), BF),
            vm((2, 3, 80, LA), BF), vm((2, 3, 80, LB), BF),
            vm((2, 4, 80, 384), BF), vm((2, 8, 80, 384), BF),
            vm((2, 4, 80, 128), BF), vm((2, 4, 80, 128), BF),
            dma((2, 4)), dma((2, 4)), dma((2, 6)), dma((2, 6)), dma((2, 3)), dma((2, 3)),
            dma((2, 3)), dma((2, 3)), dma((2, 3)), dma((2, 3)), dma((2, 4)), dma((2, 8)),
            dma((2, 8)), dma((2, 4)),
        ],
        compiler_params=pltpu.CompilerParams(
            collective_id=0, has_side_effects=True, vmem_limit_bytes=LIMIT),
        name="block_pair",
    )(timestep, qkv_weight, proj_weight, time_table, block_tables, qk_gains, u, cotangent, *rope_arrays())


def hand_over_kernel(*refs):
    for source, target in zip(refs[:6], refs[6:]):
        target[...] = source[...]


def hand_over(arrays):
    return pl.pallas_call(
        hand_over_kernel, out_shape=tuple(sds(array.shape, array.dtype) for array in arrays),
        in_specs=[VM] * 6, out_specs=(VM,) * 6, name="hand_over",
    )(*arrays)


def local(tokens, timestep, time_table, block_tables, qk_gains, qkv_weight, proj_weight, cotangent):
    frame_dev, spatial, features = tokens.shape[1:]
    shape = (1, frame_dev, spatial, features)
    count = lax.axis_size("dp") * lax.axis_size("seq") * frame_dev * spatial
    block_out, token_grad, qkv_grad, proj_grad, table_grad, gain_grad = hand_over(block_pair(
        1.0 / math.sqrt(count), timestep, jnp.swapaxes(qkv_weight, 1, 2), jnp.swapaxes(proj_weight, 1, 2),
        jnp.swapaxes(time_table, 0, 1), jnp.swapaxes(block_tables, 0, 1), qk_gains,
        tokens.reshape(288, 1152), cotangent.reshape(288, 1152)))
    return (block_out.reshape(shape), token_grad.reshape(shape), jnp.swapaxes(qkv_grad, 0, 1),
            jnp.swapaxes(proj_grad, 0, 1), jnp.swapaxes(table_grad, 0, 1), gain_grad)


def solution(mesh):
    return jax.shard_map(
        local,
        mesh=mesh,
        in_specs=(
            PS("dp", "seq", None, None),
            PS("dp"),
            PS(),
            PS(),
            PS(),
            PS(),
            PS(),
            PS("dp", "seq", None, None),
        ),
        out_specs=(
            PS("dp", "seq", None, None),
            PS("dp", "seq", None, None),
            PS(None, "seq", "dp"),
            PS(None, "seq", "dp"),
            PS(),
            PS(),
        ),
        check_vma=False,
    )
```
